128 devices in a mesh: tm: 16 (over x, y), space: 8 (over z, core).
Axes of the slice: x: 4, y: 4, z: 4, core: 2. Of those that a mesh axis runs over, the one named last changes fastest.
Arguments:
- forcing: float32 [256, 65536], P('tm', 'space'), may hold values from -6 to 6
- op_main: bfloat16 [1024, 64, 448], P('space'), may hold values from -0.1205 to 2.61
- op_mass: bfloat16 [1024, 64, 448], P('space'), may hold values from -0.0401 to 1.045
- jacobi_inv: bfloat16 [1024, 64, 64], P('space'), may hold values from -0.0301 to 0.635
Outputs:
- spec_real: float32 [256, 65536], P('tm', 'space')
- spec_imag: float32 [256, 65536], P('tm', 'space')
- time_field: float32 [256, 65536], P('tm', 'space')
The draws below stay inside these ranges and needn't reach their ends.
All inputs are finite; a program needn't handle non-finite values.
Results may differ from the reference program's by a relative error of at most 0.0058.
Values may be sent and summed in bfloat16 or wider, within the bound.
No kernel may reach another device: no remote copies, remote signals or barrier semaphores. Data moves between devices by JAX's collectives and lax.ppermute only.
A program may use at most 128 MiB of HBM per device.

```python
import math
import jax
import jax.numpy as jnp
from jax import lax

L = 256
BS = 64
BX = 4
BY = 4
NZ = 64
NBLK = 1024
NDOF = 65536


def block_draw(key, slot_count, diag_low, diag_high, near_bound, far_bound):
    key_diag, key_near, key_far = jax.random.split(key, 3)
    full_shape = (NBLK, BS, slot_count * BS)
    near_jitter = jax.random.uniform(key_near, full_shape, minval=-near_bound, maxval=near_bound)
    far_jitter = jax.random.uniform(key_far, full_shape, minval=-far_bound, maxval=far_bound)
    diag_values = jax.random.uniform(key_diag, (NBLK, BS), minval=diag_low, maxval=diag_high)
    column = lax.broadcasted_iota(jnp.int32, full_shape, 2)
    output_row = lax.broadcasted_iota(jnp.int32, full_shape, 1)
    jitter = jnp.where(column < BS, near_jitter, far_jitter)
    return jitter + jnp.where(column == output_row, diag_values[:, :, None], 0.0)


def draw_op_main(key, part):
    values = block_draw(jax.random.fold_in(key, 11), 7, 1.5, 2.5, 0.1, 0.12)
    return values.astype(jnp.bfloat16)


def draw_op_mass(key, part):
    values = block_draw(jax.random.fold_in(key, 12), 7, 0.5, 1.0, 0.04, 0.04)
    return values.astype(jnp.bfloat16)


def draw_jacobi_inv(key, part):
    values = block_draw(jax.random.fold_in(key, 13), 1, 0.3, 0.6, 0.03, 0.03)
    return values.astype(jnp.bfloat16)


def levels(stream_key, dims, pieces, smallest, largest):
    gain, own = 1.0, jax.random.fold_in(stream_key, 6)
    for axis_at, parts in pieces:
        heights = jnp.exp(jax.random.uniform(jax.random.fold_in(own, axis_at), (parts,), jnp.float32, smallest / len(pieces), largest / len(pieces)))
        gain = gain * jnp.repeat(heights, dims[axis_at] // parts).reshape([-1 if axis == axis_at else 1 for axis in range(len(dims))])
    return gain


def gaussian(rng, extent, spread, reach, cuts=(), kind=jnp.bfloat16):
    entries = jax.random.normal(rng, extent, jnp.float32) * spread
    if len(cuts) > 0:
        entries = levels(rng, extent, cuts, -0.22, 0.18) * entries
    return jnp.clip(entries, min=-reach, max=reach).astype(kind)


def setup_inputs(seed: int = 0) -> dict:
    key_list = jax.random.split(jax.random.key(seed), 5)
    return {
        "forcing": gaussian(key_list[0], (L, NDOF), 1.0, 6.0, ((0, 16), (1, 8)), jnp.float32),
        "op_main": draw_op_main(jax.random.fold_in(key_list[4], 71), 0),
        "op_mass": draw_op_mass(jax.random.fold_in(key_list[4], 71), 0),
        "jacobi_inv": draw_jacobi_inv(jax.random.fold_in(key_list[4], 71), 0),
    }


alpha_decay = 0.25
two_pi = 2.0 * math.pi


def neighbour_stack(field_low):
    row_count = field_low.shape[0]
    shaped = field_low.reshape(row_count, NZ, BY, BX, BS)
    padded = jnp.pad(shaped, ((0, 0), (1, 1), (1, 1), (1, 1), (0, 0)))
    neighbours = [
        padded[:, 1:-1, 1:-1, 1:-1],
        padded[:, 1:-1, 1:-1, :-2],
        padded[:, 1:-1, 1:-1, 2:],
        padded[:, 1:-1, :-2, 1:-1],
        padded[:, 1:-1, 2:, 1:-1],
        padded[:, :-2, 1:-1, 1:-1],
        padded[:, 2:, 1:-1, 1:-1],
    ]
    return jnp.stack(neighbours, axis=4).reshape(row_count, NBLK, 7 * BS)


def apply_block(matrix, field_low):
    row_count = field_low.shape[0]
    stacked = neighbour_stack(field_low)
    product = jnp.einsum("bok,rbk->rbo", matrix, stacked, precision=lax.Precision.HIGHEST)
    return product.reshape(row_count, NDOF)


def apply_inverse(matrix, field_low):
    row_count = field_low.shape[0]
    shaped = field_low.reshape(row_count, NBLK, BS)
    product = jnp.einsum("boi,rbi->rbo", matrix, shaped, precision=lax.Precision.HIGHEST)
    return product.reshape(row_count, NDOF)


def to_low(values):
    rounded = values.astype(jnp.bfloat16)
    rounded = lax.optimization_barrier(rounded)
    return rounded.astype(jnp.float32)


def reference(forcing, op_main, op_mass, jacobi_inv):
    step_ids = jnp.arange(L, dtype=jnp.int32)
    ratios = step_ids.astype(jnp.float32) / L
    scaled = forcing * jnp.power(jnp.float32(alpha_decay), ratios)[:, None]
    spectrum = jnp.fft.fft(scaled, axis=0, norm="ortho")
    rhs_parts = jnp.stack([jnp.real(spectrum), jnp.imag(spectrum)], axis=1).astype(jnp.float32)
    phases = step_ids.astype(jnp.float32) * (-two_pi / L)
    modulus = alpha_decay ** (1.0 / L)
    beta_re = (modulus * jnp.cos(phases)).reshape(L // 8, 8)
    beta_im = (modulus * jnp.sin(phases)).reshape(L // 8, 8)
    main_wide = op_main.astype(jnp.float32)
    mass_wide = op_mass.astype(jnp.float32)
    inv_wide = jacobi_inv.astype(jnp.float32)
    grouped = rhs_parts.reshape(L // 8, 8, 2, NDOF)

    def solve_group(packed):
        rhs_group, group_re, group_im = packed
        rhs_rows = rhs_group.reshape(16, NDOF)
        first_iter = apply_inverse(inv_wide, to_low(rhs_rows))
        first_low = to_low(first_iter)
        main_image = apply_block(main_wide, first_low).reshape(8, 2, NDOF)
        mass_image = apply_block(mass_wide, first_low).reshape(8, 2, NDOF)
        coef_re = group_re[:, None]
        coef_im = group_im[:, None]
        res_re = rhs_group[:, 0] - main_image[:, 0] + coef_re * mass_image[:, 0] - coef_im * mass_image[:, 1]
        res_im = rhs_group[:, 1] - main_image[:, 1] + coef_re * mass_image[:, 1] + coef_im * mass_image[:, 0]
        residue = jnp.stack([res_re, res_im], axis=1).reshape(16, NDOF)
        second_iter = first_iter + apply_inverse(inv_wide, to_low(residue))
        return second_iter.reshape(8, 2, NDOF)

    solution = lax.map(solve_group, (grouped, beta_re, beta_im)).reshape(L, 2, NDOF)
    combined = lax.complex(solution[:, 0], solution[:, 1])
    in_time = jnp.fft.ifft(combined, axis=0, norm="ortho")
    time_field = jnp.real(in_time).astype(jnp.float32) * jnp.power(jnp.float32(alpha_decay), -ratios)[:, None]
    return solution[:, 0], solution[:, 1], time_field
```

```python
import functools
import math

import jax
import jax.numpy as jnp
import ml_dtypes
import numpy as np
from jax import lax
from jax.experimental import pallas as pl
from jax.experimental.pallas import tpu as pltpu
from jax.sharding import PartitionSpec as P

LENGTH = 256
PARTS = 16
STEPS = LENGTH // PARTS
BS = 64
LAYER = 1024
ROW = 256
LAYERS = 8
SLAB = LAYERS * LAYER
BLOCKS = SLAB // BS
SLOTS = 7
COL = 128
OWN = 4 * COL
BOX = 12 * COL
CHUNK = 16

ALPHA = 0.25
LOG_STEP = math.log(ALPHA) / LENGTH
MODULUS = ALPHA ** (1.0 / LENGTH)

f32 = jnp.float32
bf16 = jnp.bfloat16


def box_of(part):
    return part // 4, part // 2 % 2, part % 2


def dft_table():
    freq = np.arange(LENGTH)[:, None]
    step = np.arange(LENGTH)[None, :]
    angle = 2.0 * np.pi * (freq * step % LENGTH) / LENGTH
    table = np.stack([np.cos(angle), -np.sin(angle)], 1) / math.sqrt(LENGTH)
    table = table.reshape(PARTS, STEPS, 2, LENGTH).transpose(0, 2, 1, 3)
    table = table.reshape(2 * LENGTH, LENGTH)
    high = table.astype(ml_dtypes.bfloat16)
    low = (table - high.astype(np.float64)).astype(ml_dtypes.bfloat16)
    return np.concatenate([high, high, low], axis=1)


def step_ids(part, count, width):
    return part * STEPS + lax.broadcasted_iota(jnp.int32, (count, width), 0)


def cost(flops, nbytes):
    return pl.CostEstimate(flops=flops, bytes_accessed=nbytes, transcendentals=0)


def dot(a, b):
    return jnp.dot(a, b, preferred_element_type=f32)


def pack_kernel(forcing, low_edge, high_edge, out):
    part = lax.axis_index("tm")
    ids = step_ids(part, STEPS, COL).astype(f32)
    scale = jnp.exp(ids * LOG_STEP)
    half = lax.broadcasted_iota(jnp.int32, (STEPS, COL), 1) < BS
    cols = {}

    def column(z, y, x):
        at = z * LAYER + y * ROW + x * COL
        if at not in cols:
            cols[at] = forcing[:, at : at + COL] * scale
        return cols[at]

    def put(dest, c, value):
        out[dest, :, c * COL : (c + 1) * COL] = value.astype(bf16)

    for dest in range(PARTS):
        zg, yg, xg = box_of(dest)
        for d in range(2):
            for e in range(2):
                put(dest, 2 * d + e, column(2 * zg + d, 2 * yg + e, xg))
            y = 2 * yg + d
            at = y * ROW + xg * COL
            if zg == 0:
                put(dest, 4 + d, low_edge[:, at : at + COL])
            else:
                put(dest, 4 + d, column(2 * zg - 1, y, xg))
            if zg == 3:
                put(dest, 6 + d, high_edge[:, at : at + COL])
            else:
                put(dest, 6 + d, column(2 * zg + 2, y, xg))
            z = 2 * zg + d
            put(dest, 8 + d, column(z, 2 - yg, xg))
            first = column(z, 2 * yg, 1 - xg)
            second = column(z, 2 * yg + 1, 1 - xg)
            if xg == 0:
                pair = jnp.where(half, first, pltpu.roll(second, BS, 1))
            else:
                pair = jnp.where(half, pltpu.roll(first, BS, 1), second)
            put(dest, 10 + d, pair)


def pack(forcing, low_edge, high_edge):
    return pl.pallas_call(
        pack_kernel,
        out_shape=jax.ShapeDtypeStruct((PARTS, STEPS, BOX), bf16),
        name="pack",
        cost_estimate=cost(10**6, 2 * 10**6),
    )(forcing, low_edge, high_edge)


def selector(blocks, width):
    block = lax.broadcasted_iota(jnp.int32, (BLOCKS, width), 0)
    lane = lax.broadcasted_iota(jnp.int32, (BLOCKS, width), 1)
    hit = block == blocks
    pieces = [
        jnp.where(hit & (lane % CHUNK == o), 1.0, 0.0).astype(bf16) for o in range(CHUNK)
    ]
    return jnp.concatenate(pieces, axis=0)


def reorder(width):
    slots = width // BS
    source = lax.broadcasted_iota(jnp.int32, (width, width), 0)
    lane = lax.broadcasted_iota(jnp.int32, (width, width), 1)
    wanted = lane % BS // CHUNK * (slots * CHUNK) + lane // BS * CHUNK + lane % CHUNK
    return jnp.where(source == wanted, 1.0, 0.0).astype(bf16)


def select_chunk(read, chosen):
    rows = jnp.concatenate([read(o) for o in range(CHUNK)], axis=1)
    return dot(rows, chosen).astype(bf16)


def jac_blocks(slot, zg, yg, xg):
    c = slot // 2
    e = slot % 2
    d = c % 2
    kind = c // 2

    def block(z, y, x):
        return z * 16 + y * 4 + x

    own = block(2 * zg + kind % 2, 2 * yg + d, 2 * xg + e)
    below = block(jnp.maximum(2 * zg - 1, 0), 2 * yg + d, 2 * xg + e)
    above = block(jnp.minimum(2 * zg + 2, LAYERS - 1), 2 * yg + d, 2 * xg + e)
    beside = block(2 * zg + d, 2 - yg, 2 * xg + e)
    ahead = block(2 * zg + d, 2 * yg + e, 2 - xg)
    top = block(LAYERS - 1, 2 * yg + d, 2 * xg + e)
    bottom = block(0, 2 * yg + d, 2 * xg + e)
    result = own
    for at, choice in enumerate([below, above, beside, ahead, top, bottom]):
        result = jnp.where(kind == at + 2, choice, result)
    return result


def jac_kernel(jac, box, top, bottom):
    zg, yg, xg = box_of(lax.axis_index("tm"))
    width = 2 * COL
    perm = reorder(4 * width)
    tiles = []
    for tile in range(2):
        lane = lax.broadcasted_iota(jnp.int32, (1, width), 1)
        chosen = selector(jac_blocks(tile * 16 + lane // CHUNK, zg, yg, xg), width)
        chunks = [
            select_chunk(lambda o: jac[c * CHUNK + o], chosen) for c in range(BS // CHUNK)
        ]
        tiles.append(dot(jnp.concatenate(chunks, axis=1), perm).astype(bf16))
    box[:, : 8 * COL] = tiles[0]
    box[:, 8 * COL :] = tiles[1][:, : 4 * COL]
    top[...] = tiles[1][:, 4 * COL : 6 * COL]
    bottom[...] = tiles[1][:, 6 * COL :]


def select_jac(jac):
    edge = jax.ShapeDtypeStruct((BS, 2 * COL), bf16)
    return pl.pallas_call(
        jac_kernel,
        out_shape=(jax.ShapeDtypeStruct((BS, BOX), bf16), edge, edge),
        name="select_jac",
        cost_estimate=cost(10**9, 2 * 10**6),
    )(jac)


def ops_kernel(main, mass, out, chosen, picked):
    step = pl.program_id(0)
    zg, yg, xg = box_of(lax.axis_index("tm"))

    @pl.when(step == 0)
    def _():
        lane = lax.broadcasted_iota(jnp.int32, (1, COL), 1)
        slot = lane // CHUNK
        blocks = (
            (2 * zg + slot // 4) * 16 + (2 * yg + slot // 2 % 2) * 4 + 2 * xg + slot % 2
        )
        chosen[...] = selector(blocks, COL)

    for which, source in enumerate((main, mass)):
        picked[which, step] = select_chunk(lambda o: source[o], chosen[...])

    @pl.when(step == BS // CHUNK - 1)
    def _():
        perm = reorder(4 * COL)
        both = [
            dot(
                jnp.concatenate([picked[which, c] for c in range(BS // CHUNK)], axis=1), perm
            )
            for which in range(2)
        ]
        lane = lax.broadcasted_iota(jnp.int32, (BS, 2 * COL), 1)
        low = lane % COL < BS
        zero = jnp.zeros((BS, 2 * COL), f32)
        for dz in range(2):
            for dy in range(2):
                pair = 2 * dz + dy
                cut = slice(pair * COL, (pair + 1) * COL)
                slots = [
                    jnp.concatenate([b[s * BS : (s + 1) * BS, cut] for b in both], axis=1)
                    for s in range(SLOTS)
                ]

                def put(at, value):
                    out[pair, at * BS : (at + 1) * BS] = value.astype(bf16)

                def diagonal(at, value):
                    put(at, jnp.where(low, value, zero))
                    put(at + 1, jnp.where(low, zero, value))

                put(0, jnp.where(low, slots[0], slots[1]))
                put(1, jnp.where(low, slots[2], slots[0]))
                diagonal(2, slots[6 - dz])
                diagonal(4, slots[4 - dy])
                diagonal(6, slots[5 + dz])
                faces = (yg == 1) if dy == 0 else (yg == 0)
                diagonal(8, slots[3 + dy] * jnp.where(faces, 1.0, 0.0))
                after = jnp.where(xg == 0, 1.0, 0.0)
                put(
                    10 + dy,
                    jnp.where(low, slots[1] * (1.0 - after), slots[2] * after),
                )
                put(11 - dy, zero)


def select_ops(main, mass):
    spec = pl.BlockSpec((CHUNK, SLOTS * BS, BLOCKS), lambda c: (c, 0, 0))
    return pl.pallas_call(
        ops_kernel,
        grid=(BS // CHUNK,),
        in_specs=[spec, spec],
        out_specs=pl.BlockSpec((4, 6 * COL, 2 * COL), lambda c: (0, 0, 0)),
        out_shape=jax.ShapeDtypeStruct((4, 6 * COL, 2 * COL), bf16),
        scratch_shapes=[
            pltpu.VMEM((CHUNK * BLOCKS, COL), bf16),
            pltpu.VMEM((2, BS // CHUNK, SLOTS * BS, COL), bf16),
        ],
        name="select_ops",
        compiler_params=pltpu.CompilerParams(vmem_limit_bytes=40 * 2**20),
        cost_estimate=cost(4 * 10**9, 16 * 10**6),
    )(main, mass)


def solve_kernel(recv, ops, box, from_low, from_high, table, out):
    zg, _, _ = box_of(lax.axis_index("tm"))
    low = lax.broadcasted_iota(jnp.int32, (BS, COL), 1) < BS
    zero = jnp.zeros((BS, COL), bf16)

    def fields(c):
        return recv[:, c * COL : (c + 1) * COL]

    def inverse(c):
        value = box[:, c * COL : (c + 1) * COL]
        if c in (4, 5):
            value = jnp.where(zg == 0, from_low[:, (c - 4) * COL : (c - 3) * COL], value)
        if c in (6, 7):
            value = jnp.where(zg == 3, from_high[:, (c - 6) * COL : (c - 5) * COL], value)
        return jnp.concatenate(
            [jnp.where(low, value, zero), jnp.where(low, zero, value)], axis=0
        )

    inverses = [inverse(c) for c in range(4)]
    firsts = [dot(fields(c), inverses[c]) for c in range(4)]
    lows = [value.astype(bf16) for value in firsts]
    lows += [dot(fields(c), inverse(c)).astype(bf16) for c in range(4, 12)]

    ids = step_ids(0, LENGTH, COL).astype(f32)
    growth = jnp.exp(ids * -LOG_STEP)
    seconds = []
    for dz in range(2):
        for dy in range(2):
            pair = 2 * dz + dy
            around = jnp.concatenate(
                [
                    lows[pair],
                    lows[2 - 2 * dz + dy],
                    lows[2 * dz + 1 - dy],
                    lows[4 + 2 * dz + dy],
                    lows[8 + dz],
                    lows[10 + dz],
                ],
                axis=1,
            )
            image = dot(around, ops[pair])
            earlier = pltpu.roll(image[:, COL:], 1, 0)
            residue = fields(pair).astype(f32) - image[:, :COL] + MODULUS * earlier
            second = firsts[pair] + dot(residue.astype(bf16), inverses[pair])
            in_time = (second * growth).astype(bf16)
            for dest in range(PARTS):
                out[dest, 2 * STEPS :, pair * COL : (pair + 1) * COL] = in_time[
                    dest * STEPS : (dest + 1) * STEPS
                ]
            seconds.append(second)
    second = jnp.concatenate(seconds, axis=1)
    high = second.astype(bf16)
    rest = (second - high.astype(f32)).astype(bf16)
    spectrum = dot(table[...], jnp.concatenate([high, rest, high], axis=0)).astype(bf16)
    for dest in range(PARTS):
        out[dest, : 2 * STEPS] = spectrum[dest * 2 * STEPS : (dest + 1) * 2 * STEPS]


def solve(recv, ops, box, from_low, from_high):
    return pl.pallas_call(
        solve_kernel,
        out_shape=jax.ShapeDtypeStruct((PARTS, 3 * STEPS, OWN), bf16),
        name="solve",
        compiler_params=pltpu.CompilerParams(vmem_limit_bytes=40 * 2**20),
        cost_estimate=cost(3 * 10**9, 5 * 10**6),
    )(recv, ops, box, from_low, from_high, jnp.asarray(dft_table()))


def unpack_kernel(recv, real, imag, in_time):
    for source in range(PARTS):
        zg, yg, xg = box_of(source)
        for d in range(2):
            for e in range(2):
                at = (2 * zg + d) * LAYER + (2 * yg + e) * ROW + xg * COL
                c = 2 * d + e
                for which, out in enumerate((real, imag, in_time)):
                    out[:, at : at + COL] = recv[
                        source,
                        which * STEPS : (which + 1) * STEPS,
                        c * COL : (c + 1) * COL,
                    ].astype(f32)


def unpack(recv):
    out = jax.ShapeDtypeStruct((STEPS, SLAB), f32)
    return pl.pallas_call(
        unpack_kernel,
        out_shape=(out, out, out),
        name="unpack",
        cost_estimate=cost(10**6, 3 * 10**6),
    )(recv)


def per_device(forcing, op_main, op_mass, jacobi_inv):
    count = lax.axis_size("space")
    up = [(i, i + 1) for i in range(count - 1)]
    down = [(i + 1, i) for i in range(count - 1)]
    local_ids = lax.axis_index("tm") * STEPS + jnp.arange(STEPS, dtype=jnp.int32)
    scale = jnp.exp(local_ids.astype(f32) * LOG_STEP)[:, None]
    bottom = (forcing[:, :LAYER] * scale).astype(bf16)
    top = (forcing[:, SLAB - LAYER :] * scale).astype(bf16)
    low_edge = lax.ppermute(top, "space", up)
    high_edge = lax.ppermute(bottom, "space", down)

    box, jac_top, jac_bottom = select_jac(jnp.transpose(jacobi_inv, (1, 2, 0)))
    packed = pack(forcing, low_edge, high_edge)
    packed, jac_top, jac_bottom = lax.optimization_barrier((packed, jac_top, jac_bottom))
    recv = lax.all_to_all(packed, "tm", 0, 0).reshape(LENGTH, BOX)
    from_low = lax.ppermute(jac_top, "space", up)
    from_high = lax.ppermute(jac_bottom, "space", down)
    ops = select_ops(jnp.transpose(op_main, (1, 2, 0)), jnp.transpose(op_mass, (1, 2, 0)))
    sent = solve(recv, ops, box, from_low, from_high)
    back = lax.all_to_all(sent, "tm", 0, 0)
    return unpack(back)


def solution(mesh):
    in_specs = (
        P("tm", "space"),
        P("space", None, None),
        P("space", None, None),
        P("space", None, None),
    )
    out_specs = (P("tm", "space"), P("tm", "space"), P("tm", "space"))
    return jax.shard_map(
        per_device, mesh=mesh, in_specs=in_specs, out_specs=out_specs, check_vma=False
    )
```

```python
import functools
import math

import jax
import jax.numpy as jnp
import ml_dtypes
import numpy as np
from jax import lax
from jax.experimental import pallas as pl
from jax.experimental.pallas import tpu as pltpu
from jax.sharding import PartitionSpec as P

LENGTH = 256
PARTS = 16
STEPS = LENGTH // PARTS
BS = 64
LAYER = 1024
ROW = 256
LAYERS = 8
SLAB = LAYERS * LAYER
BLOCKS = SLAB // BS
SLOTS = 7
COL = 128
OWN = 4 * COL
BOX = 12 * COL
CHUNK = 16

ALPHA = 0.25
LOG_STEP = math.log(ALPHA) / LENGTH
MODULUS = ALPHA ** (1.0 / LENGTH)

f32 = jnp.float32
bf16 = jnp.bfloat16


def box_of(part):
    return part // 4, part // 2 % 2, part % 2


def dft_table():
    freq = np.arange(LENGTH)[:, None]
    step = np.arange(LENGTH)[None, :]
    angle = 2.0 * np.pi * (freq * step % LENGTH) / LENGTH
    table = np.stack([np.cos(angle), -np.sin(angle)], 1) / math.sqrt(LENGTH)
    table = table.reshape(PARTS, STEPS, 2, LENGTH).transpose(0, 2, 1, 3)
    table = table.reshape(2 * LENGTH, LENGTH)
    high = table.astype(ml_dtypes.bfloat16)
    low = (table - high.astype(np.float64)).astype(ml_dtypes.bfloat16)
    return np.concatenate([high, high, low], axis=1)


def step_ids(part, count, width):
    return part * STEPS + lax.broadcasted_iota(jnp.int32, (count, width), 0)


def cost(flops, nbytes):
    return pl.CostEstimate(flops=flops, bytes_accessed=nbytes, transcendentals=0)


def dot(a, b):
    return jnp.dot(a, b, preferred_element_type=f32)


def scales():
    ids = step_ids(lax.axis_index("tm"), STEPS, COL).astype(f32)
    return jnp.exp(ids * LOG_STEP)


def pack_kernel(source, out, forcing, sems):
    copies = []
    for group in range(4):
        cut = pl.ds(group * 2 * LAYER, 2 * LAYER)
        copies.append(
            pltpu.make_async_copy(source.at[:, cut], forcing.at[:, cut], sems.at[group])
        )
    for copy in copies:
        copy.start()
    for copy in copies:
        copy.wait()
    scale = scales()
    half = lax.broadcasted_iota(jnp.int32, (STEPS, COL), 1) < BS

    def column(z, y, x):
        at = z * LAYER + y * ROW + x * COL
        return forcing[:, at : at + COL] * scale

    def put(dest, c, value):
        out[dest, :, c * COL : (c + 1) * COL] = value.astype(bf16)

    for dest in range(PARTS):
        zg, yg, xg = box_of(dest)
        for d in range(2):
            for e in range(2):
                put(dest, 2 * d + e, column(2 * zg + d, 2 * yg + e, xg))
            y = 2 * yg + d
            if zg > 0:
                put(dest, 4 + d, column(2 * zg - 1, y, xg))
            if zg < 3:
                put(dest, 6 + d, column(2 * zg + 2, y, xg))
            z = 2 * zg + d
            put(dest, 8 + d, column(z, 2 - yg, xg))
            first = column(z, 2 * yg, 1 - xg)
            second = column(z, 2 * yg + 1, 1 - xg)
            if xg == 0:
                pair = jnp.where(half, first, pltpu.roll(second, BS, 1))
            else:
                pair = jnp.where(half, pltpu.roll(first, BS, 1), second)
            put(dest, 10 + d, pair)


def pack(forcing):
    return pl.pallas_call(
        pack_kernel,
        in_specs=[pl.BlockSpec(memory_space=pltpu.HBM)],
        out_shape=jax.ShapeDtypeStruct((PARTS, STEPS, BOX), bf16),
        scratch_shapes=[pltpu.VMEM((STEPS, SLAB), f32), pltpu.SemaphoreType.DMA((4,))],
        name="pack",
        compiler_params=pltpu.CompilerParams(vmem_limit_bytes=6 * 2**20),
        cost_estimate=cost(10**6, 4 * 10**6),
    )(forcing)


def patch_kernel(packed, low_edge, high_edge, out, sems):
    copies = []
    for dest in range(PARTS):
        zg, yg, xg = box_of(dest)
        for edge, at_group, first in ((low_edge, 0, 4), (high_edge, 3, 6)):
            if zg == at_group:
                for d in range(2):
                    at = (2 * yg + d) * ROW + xg * COL
                    copies.append(
                        pltpu.make_async_copy(
                            edge.at[pl.ds(0, STEPS), pl.ds(at, COL)],
                            out.at[dest, :, pl.ds((first + d) * COL, COL)],
                            sems.at[len(copies)],
                        )
                    )
    for copy in copies:
        copy.start()
    for copy in copies:
        copy.wait()


def patch(packed, low_edge, high_edge):
    anywhere = pl.BlockSpec(memory_space=pl.ANY)
    return pl.pallas_call(
        patch_kernel,
        in_specs=[anywhere] * 3,
        out_specs=anywhere,
        out_shape=jax.ShapeDtypeStruct((PARTS, STEPS, BOX), bf16),
        scratch_shapes=[pltpu.SemaphoreType.DMA((16,))],
        input_output_aliases={0: 0},
        name="patch",
        compiler_params=pltpu.CompilerParams(vmem_limit_bytes=2**20),
        cost_estimate=cost(10**3, 2 * 10**5),
    )(packed, low_edge, high_edge)


def selector(blocks, width):
    block = lax.broadcasted_iota(jnp.int32, (BLOCKS, width), 0)
    lane = lax.broadcasted_iota(jnp.int32, (BLOCKS, width), 1)
    hit = block == blocks
    pieces = [
        jnp.where(hit & (lane % CHUNK == o), 1.0, 0.0).astype(bf16) for o in range(CHUNK)
    ]
    return jnp.concatenate(pieces, axis=0)


def reorder(width):
    slots = width // BS
    source = lax.broadcasted_iota(jnp.int32, (width, width), 0)
    lane = lax.broadcasted_iota(jnp.int32, (width, width), 1)
    wanted = lane % BS // CHUNK * (slots * CHUNK) + lane // BS * CHUNK + lane % CHUNK
    return jnp.where(source == wanted, 1.0, 0.0).astype(bf16)


def select_chunk(read, chosen):
    rows = jnp.concatenate([read(o) for o in range(CHUNK)], axis=1)
    return dot(rows, chosen).astype(bf16)


def select_all(jac, blocks, perm):
    chunks = BS // CHUNK
    rows = jnp.concatenate(
        [
            jnp.concatenate([jac[c * CHUNK + o] for c in range(chunks)], axis=0)
            for o in range(CHUNK)
        ],
        axis=1,
    )
    picked = dot(rows, selector(blocks, COL)).astype(bf16)
    side = jnp.concatenate([picked[c * BS : (c + 1) * BS] for c in range(chunks)], axis=1)
    return dot(side, perm).astype(bf16)


def slots_of():
    return lax.broadcasted_iota(jnp.int32, (1, COL), 1) // CHUNK


def block_at(z, y, x):
    return z * 16 + y * 4 + x


def edge_kernel(forcing, jac, top, bottom, ends, local, sems):
    copies = [
        pltpu.make_async_copy(jac, local, sems.at[0]),
        pltpu.make_async_copy(forcing.at[:, pl.ds(0, LAYER)], ends.at[0], sems.at[1]),
        pltpu.make_async_copy(
            forcing.at[:, pl.ds(SLAB - LAYER, LAYER)], ends.at[1], sems.at[2]
        ),
    ]
    for copy in copies:
        copy.start()
    _, yg, xg = box_of(lax.axis_index("tm"))
    scale = jnp.concatenate([scales()] * (LAYER // COL), axis=1)
    slot = slots_of()
    layer = jnp.where(slot < 4, LAYERS - 1, 0)
    blocks = block_at(layer, 2 * yg + slot // 2 % 2, 2 * xg + slot % 2)
    perm = reorder(4 * COL)
    for copy in copies:
        copy.wait()
    bottom[:STEPS] = (ends[0] * scale).astype(bf16)
    top[:STEPS] = (ends[1] * scale).astype(bf16)
    picked = select_all(local, blocks, perm)
    for a in range(BS // STEPS):
        cut = slice(a * 2 * COL, (a + 1) * 2 * COL)
        top[STEPS:, cut] = picked[a * STEPS : (a + 1) * STEPS, : 2 * COL]
        bottom[STEPS:, cut] = picked[a * STEPS : (a + 1) * STEPS, 2 * COL :]


def edges(forcing, jac):
    edge = jax.ShapeDtypeStruct((2 * STEPS, LAYER), bf16)
    hbm = pl.BlockSpec(memory_space=pltpu.HBM)
    return pl.pallas_call(
        edge_kernel,
        in_specs=[hbm, hbm],
        out_shape=(edge, edge),
        scratch_shapes=[
            pltpu.VMEM((2, STEPS, LAYER), f32),
            pltpu.VMEM((BS, BS, BLOCKS), bf16),
            pltpu.SemaphoreType.DMA((3,)),
        ],
        name="edges",
        compiler_params=pltpu.CompilerParams(vmem_limit_bytes=63 * 10**6),
        cost_estimate=cost(10**8, 2 * 10**6),
    )(forcing, jac)


def jac_kernel(jac, box, local, sem):
    copy = pltpu.make_async_copy(jac, local, sem)
    copy.start()
    zg, yg, xg = box_of(lax.axis_index("tm"))
    slot = slots_of()
    d = slot // 2 % 2
    e = slot % 2
    first = slot < 4
    own = block_at(2 * zg + slot // 4, 2 * yg + d, 2 * xg + e)
    layer = jnp.where(
        first, jnp.maximum(2 * zg - 1, 0), jnp.minimum(2 * zg + 2, LAYERS - 1)
    )
    faces = block_at(layer, 2 * yg + d, 2 * xg + e)
    beside = block_at(2 * zg + d, 2 - yg, 2 * xg + e)
    ahead = block_at(2 * zg + d, 2 * yg + e, 2 - xg)
    perm = reorder(4 * COL)
    copy.wait()
    for at, blocks in enumerate((own, faces, jnp.where(first, beside, ahead))):
        box[:, at * 4 * COL : (at + 1) * 4 * COL] = select_all(local, blocks, perm)


def select_jac(jac):
    return pl.pallas_call(
        jac_kernel,
        in_specs=[pl.BlockSpec(memory_space=pltpu.HBM)],
        out_shape=jax.ShapeDtypeStruct((BS, BOX), bf16),
        scratch_shapes=[pltpu.VMEM((BS, BS, BLOCKS), bf16), pltpu.SemaphoreType.DMA],
        name="select_jac",
        compiler_params=pltpu.CompilerParams(vmem_limit_bytes=63 * 10**6),
        cost_estimate=cost(10**9, 2 * 10**6),
    )(jac)


def ops_kernel(main, mass, out, chosen, picked):
    step = pl.program_id(0)
    zg, yg, xg = box_of(lax.axis_index("tm"))

    @pl.when(step == 0)
    def _():
        slot = slots_of()
        blocks = block_at(2 * zg + slot // 4, 2 * yg + slot // 2 % 2, 2 * xg + slot % 2)
        chosen[...] = selector(blocks, COL)

    for which, source in enumerate((main, mass)):
        picked[which, step] = select_chunk(lambda o: source[o], chosen[...])

    @pl.when(step == BS // CHUNK - 1)
    def _():
        perm = reorder(4 * COL)
        both = [
            dot(
                jnp.concatenate([picked[which, c] for c in range(BS // CHUNK)], axis=1), perm
            )
            for which in range(2)
        ]
        lane = lax.broadcasted_iota(jnp.int32, (BS, 2 * COL), 1)
        low = lane % COL < BS
        zero = jnp.zeros((BS, 2 * COL), f32)
        for dz in range(2):
            for dy in range(2):
                pair = 2 * dz + dy
                cut = slice(pair * COL, (pair + 1) * COL)
                slots = [
                    jnp.concatenate([b[s * BS : (s + 1) * BS, cut] for b in both], axis=1)
                    for s in range(SLOTS)
                ]

                def put(at, value):
                    out[pair, at * BS : (at + 1) * BS] = value.astype(bf16)

                def diagonal(at, value):
                    put(at, jnp.where(low, value, zero))
                    put(at + 1, jnp.where(low, zero, value))

                put(0, jnp.where(low, slots[0], slots[1]))
                put(1, jnp.where(low, slots[2], slots[0]))
                diagonal(2, slots[6 - dz])
                diagonal(4, slots[4 - dy])
                diagonal(6, slots[5 + dz])
                faces = (yg == 1) if dy == 0 else (yg == 0)
                diagonal(8, slots[3 + dy] * jnp.where(faces, 1.0, 0.0))
                after = jnp.where(xg == 0, 1.0, 0.0)
                put(
                    10 + dy,
                    jnp.where(low, slots[1] * (1.0 - after), slots[2] * after),
                )
                put(11 - dy, zero)


def select_ops(main, mass):
    spec = pl.BlockSpec((CHUNK, SLOTS * BS, BLOCKS), lambda c: (c, 0, 0))
    return pl.pallas_call(
        ops_kernel,
        grid=(BS // CHUNK,),
        in_specs=[spec, spec],
        out_specs=pl.BlockSpec((4, 6 * COL, 2 * COL), lambda c: (0, 0, 0)),
        out_shape=jax.ShapeDtypeStruct((4, 6 * COL, 2 * COL), bf16),
        scratch_shapes=[
            pltpu.VMEM((CHUNK * BLOCKS, COL), bf16),
            pltpu.VMEM((2, BS // CHUNK, SLOTS * BS, COL), bf16),
        ],
        name="select_ops",
        compiler_params=pltpu.CompilerParams(vmem_limit_bytes=52 * 2**20),
        cost_estimate=cost(4 * 10**9, 16 * 10**6),
    )(main, mass)


def solve_kernel(recv, ops, box, low_edge, high_edge, table, out):
    zg, _, _ = box_of(lax.axis_index("tm"))
    low = lax.broadcasted_iota(jnp.int32, (BS, COL), 1) < BS
    zero = jnp.zeros((BS, COL), bf16)

    def fields(c):
        return recv[:, c * COL : (c + 1) * COL]

    def other(edge, d):
        pieces = [
            edge[STEPS:, (2 * a + d) * COL : (2 * a + d + 1) * COL] for a in range(BS // STEPS)
        ]
        return jnp.concatenate(pieces, axis=0)

    def inverse(c):
        value = box[:, c * COL : (c + 1) * COL]
        if c in (4, 5):
            value = jnp.where(zg == 0, other(low_edge, c - 4), value)
        if c in (6, 7):
            value = jnp.where(zg == 3, other(high_edge, c - 6), value)
        return jnp.concatenate(
            [jnp.where(low, value, zero), jnp.where(low, zero, value)], axis=0
        )

    inverses = [inverse(c) for c in range(4)]
    firsts = [dot(fields(c), inverses[c]) for c in range(4)]
    lows = [value.astype(bf16) for value in firsts]
    lows += [dot(fields(c), inverse(c)).astype(bf16) for c in range(4, 12)]

    ids = step_ids(0, LENGTH, COL).astype(f32)
    growth = jnp.exp(ids * -LOG_STEP)
    seconds = []
    for dz in range(2):
        for dy in range(2):
            pair = 2 * dz + dy
            around = jnp.concatenate(
                [
                    lows[pair],
                    lows[2 - 2 * dz + dy],
                    lows[2 * dz + 1 - dy],
                    lows[4 + 2 * dz + dy],
                    lows[8 + dz],
                    lows[10 + dz],
                ],
                axis=1,
            )
            image = dot(around, ops[pair])
            earlier = pltpu.roll(image[:, COL:], 1, 0)
            residue = fields(pair).astype(f32) - image[:, :COL] + MODULUS * earlier
            second = firsts[pair] + dot(residue.astype(bf16), inverses[pair])
            in_time = (second * growth).astype(bf16)
            for dest in range(PARTS):
                out[dest, 2 * STEPS :, pair * COL : (pair + 1) * COL] = in_time[
                    dest * STEPS : (dest + 1) * STEPS
                ]
            seconds.append(second)
    second = jnp.concatenate(seconds, axis=1)
    high = second.astype(bf16)
    rest = (second - high.astype(f32)).astype(bf16)
    spectrum = dot(table[...], jnp.concatenate([high, rest, high], axis=0)).astype(bf16)
    for dest in range(PARTS):
        out[dest, : 2 * STEPS] = spectrum[dest * 2 * STEPS : (dest + 1) * 2 * STEPS]


def solve(recv, ops, box, low_edge, high_edge):
    return pl.pallas_call(
        solve_kernel,
        out_shape=jax.ShapeDtypeStruct((PARTS, 3 * STEPS, OWN), bf16),
        name="solve",
        compiler_params=pltpu.CompilerParams(vmem_limit_bytes=40 * 2**20),
        cost_estimate=cost(3 * 10**9, 5 * 10**6),
    )(recv, ops, box, low_edge, high_edge, jnp.asarray(dft_table()))


def unpack_kernel(recv, real, imag, in_time, ready, sems):
    copies = []
    for zg in range(4):
        for which, out in enumerate((real, imag, in_time)):
            for d in range(2):
                for rest in range(4):
                    source = 4 * zg + rest
                    _, yg, xg = box_of(source)
                    for e in range(2):
                        at = (2 * zg + d) * LAYER + (2 * yg + e) * ROW + xg * COL
                        c = 2 * d + e
                        ready[which, :, at : at + COL] = recv[
                            source,
                            which * STEPS : (which + 1) * STEPS,
                            c * COL : (c + 1) * COL,
                        ].astype(f32)
            cut = pl.ds(2 * zg * LAYER, 2 * LAYER)
            copy = pltpu.make_async_copy(
                ready.at[which, :, cut], out.at[:, cut], sems.at[len(copies)]
            )
            copy.start()
            copies.append(copy)
    for copy in copies:
        copy.wait()


def unpack(recv):
    out = jax.ShapeDtypeStruct((STEPS, SLAB), f32)
    return pl.pallas_call(
        unpack_kernel,
        out_shape=(out, out, out),
        out_specs=(pl.BlockSpec(memory_space=pltpu.HBM),) * 3,
        scratch_shapes=[pltpu.VMEM((3, STEPS, SLAB), f32), pltpu.SemaphoreType.DMA((12,))],
        name="unpack",
        compiler_params=pltpu.CompilerParams(vmem_limit_bytes=6 * 2**20),
        cost_estimate=cost(10**6, 3 * 10**6),
    )(recv)


def per_device(forcing, op_main, op_mass, jacobi_inv):
    count = lax.axis_size("space")
    up = [(i, i + 1) for i in range(count - 1)]
    down = [(i + 1, i) for i in range(count - 1)]
    jac = jnp.transpose(jacobi_inv, (1, 2, 0))
    top, bottom = edges(forcing, jac)
    low_edge = lax.ppermute(top, "space", up)
    high_edge = lax.ppermute(bottom, "space", down)
    packed = pack(forcing)
    low_edge, high_edge, packed = lax.optimization_barrier((low_edge, high_edge, packed))
    packed = patch(packed, low_edge, high_edge)
    packed, jac, op_main, op_mass = lax.optimization_barrier((packed, jac, op_main, op_mass))
    recv = lax.all_to_all(packed, "tm", 0, 0).reshape(LENGTH, BOX)
    box = select_jac(jac)
    ops = select_ops(jnp.transpose(op_main, (1, 2, 0)), jnp.transpose(op_mass, (1, 2, 0)))
    sent = solve(recv, ops, box, low_edge, high_edge)
    back = lax.all_to_all(sent, "tm", 0, 0)
    return unpack(back)


def solution(mesh):
    in_specs = (
        P("tm", "space"),
        P("space", None, None),
        P("space", None, None),
        P("space", None, None),
    )
    out_specs = (P("tm", "space"), P("tm", "space"), P("tm", "space"))
    return jax.shard_map(
        per_device, mesh=mesh, in_specs=in_specs, out_specs=out_specs, check_vma=False
    )
```

```python
import functools
import math

import jax
import jax.numpy as jnp
import ml_dtypes
import numpy as np
from jax import lax
from jax.experimental import pallas as pl
from jax.experimental.pallas import tpu as pltpu
from jax.sharding import PartitionSpec as P

LENGTH = 256
PARTS = 16
STEPS = LENGTH // PARTS
BS = 64
LAYER = 1024
ROW = 256
LAYERS = 8
SLAB = LAYERS * LAYER
BLOCKS = SLAB // BS
SLOTS = 7
COL = 128
OWN = 4 * COL
BOX = 12 * COL
CHUNK = 16

ALPHA = 0.25
LOG_STEP = math.log(ALPHA) / LENGTH
MODULUS = ALPHA ** (1.0 / LENGTH)

f32 = jnp.float32
bf16 = jnp.bfloat16


def box_of(part):
    return part // 4, part // 2 % 2, part % 2


def dft_table():
    freq = np.arange(LENGTH)[:, None]
    step = np.arange(LENGTH)[None, :]
    angle = 2.0 * np.pi * (freq * step % LENGTH) / LENGTH
    table = np.stack([np.cos(angle), -np.sin(angle)], 1) / math.sqrt(LENGTH)
    table = table.reshape(PARTS, STEPS, 2, LENGTH).transpose(0, 2, 1, 3)
    table = table.reshape(2 * LENGTH, LENGTH)
    high = table.astype(ml_dtypes.bfloat16)
    low = (table - high.astype(np.float64)).astype(ml_dtypes.bfloat16)
    return np.concatenate([high, high, low], axis=1)


def step_ids(part, count, width):
    return part * STEPS + lax.broadcasted_iota(jnp.int32, (count, width), 0)


def cost(flops, nbytes):
    return pl.CostEstimate(flops=flops, bytes_accessed=nbytes, transcendentals=0)


def dot(a, b):
    return jnp.dot(a, b, preferred_element_type=f32)


def scales():
    ids = step_ids(lax.axis_index("tm"), STEPS, COL).astype(f32)
    return jnp.exp(ids * LOG_STEP)


def pack_kernel(source, out, forcing, sems):
    copies = []
    for group in range(4):
        cut = pl.ds(group * 2 * LAYER, 2 * LAYER)
        copies.append(
            pltpu.make_async_copy(source.at[:, cut], forcing.at[:, cut], sems.at[group])
        )
    for copy in copies:
        copy.start()
    for copy in copies:
        copy.wait()
    scale = scales()
    half = lax.broadcasted_iota(jnp.int32, (STEPS, COL), 1) < BS

    def column(z, y, x):
        at = z * LAYER + y * ROW + x * COL
        return forcing[:, at : at + COL] * scale

    def put(dest, c, value):
        out[dest, :, c * COL : (c + 1) * COL] = value.astype(bf16)

    for dest in range(PARTS):
        zg, yg, xg = box_of(dest)
        for d in range(2):
            for e in range(2):
                put(dest, 2 * d + e, column(2 * zg + d, 2 * yg + e, xg))
            y = 2 * yg + d
            if zg > 0:
                put(dest, 4 + d, column(2 * zg - 1, y, xg))
            if zg < 3:
                put(dest, 6 + d, column(2 * zg + 2, y, xg))
            z = 2 * zg + d
            put(dest, 8 + d, column(z, 2 - yg, xg))
            first = column(z, 2 * yg, 1 - xg)
            second = column(z, 2 * yg + 1, 1 - xg)
            if xg == 0:
                pair = jnp.where(half, first, pltpu.roll(second, BS, 1))
            else:
                pair = jnp.where(half, pltpu.roll(first, BS, 1), second)
            put(dest, 10 + d, pair)


def pack(forcing):
    return pl.pallas_call(
        pack_kernel,
        in_specs=[pl.BlockSpec(memory_space=pltpu.HBM)],
        out_shape=jax.ShapeDtypeStruct((PARTS, STEPS, BOX), bf16),
        scratch_shapes=[pltpu.VMEM((STEPS, SLAB), f32), pltpu.SemaphoreType.DMA((4,))],
        name="pack",
        compiler_params=pltpu.CompilerParams(vmem_limit_bytes=6 * 2**20),
        cost_estimate=cost(10**6, 4 * 10**6),
    )(forcing)


def patch_kernel(packed, near, far, out, sems):
    def place(low_edge, high_edge):
        copies = []
        for dest in range(PARTS):
            zg, yg, xg = box_of(dest)
            for edge, at_group, first in ((low_edge, 0, 4), (high_edge, 3, 6)):
                if zg == at_group:
                    for d in range(2):
                        at = (2 * yg + d) * ROW + xg * COL
                        copies.append(
                            pltpu.make_async_copy(
                                edge.at[pl.ds(0, STEPS), pl.ds(at, COL)],
                                out.at[dest, :, pl.ds((first + d) * COL, COL)],
                                sems.at[len(copies)],
                            )
                        )
        for copy in copies:
            copy.start()
        for copy in copies:
            copy.wait()

    core = lax.axis_index("space") % 2

    @pl.when(core == 0)
    def _():
        place(far, near)

    @pl.when(core == 1)
    def _():
        place(near, far)


def patch(packed, near, far):
    anywhere = pl.BlockSpec(memory_space=pl.ANY)
    return pl.pallas_call(
        patch_kernel,
        in_specs=[anywhere] * 3,
        out_specs=anywhere,
        out_shape=jax.ShapeDtypeStruct((PARTS, STEPS, BOX), bf16),
        scratch_shapes=[pltpu.SemaphoreType.DMA((16,))],
        input_output_aliases={0: 0},
        name="patch",
        compiler_params=pltpu.CompilerParams(vmem_limit_bytes=2**20),
        cost_estimate=cost(10**3, 2 * 10**5),
    )(packed, near, far)


def selector(blocks, width):
    block = lax.broadcasted_iota(jnp.int32, (BLOCKS, width), 0)
    lane = lax.broadcasted_iota(jnp.int32, (BLOCKS, width), 1)
    hit = block == blocks
    pieces = [
        jnp.where(hit & (lane % CHUNK == o), 1.0, 0.0).astype(bf16) for o in range(CHUNK)
    ]
    return jnp.concatenate(pieces, axis=0)


def reorder(width):
    slots = width // BS
    source = lax.broadcasted_iota(jnp.int32, (width, width), 0)
    lane = lax.broadcasted_iota(jnp.int32, (width, width), 1)
    wanted = lane % BS // CHUNK * (slots * CHUNK) + lane // BS * CHUNK + lane % CHUNK
    return jnp.where(source == wanted, 1.0, 0.0).astype(bf16)


def select_chunk(read, chosen):
    rows = jnp.concatenate([read(o) for o in range(CHUNK)], axis=1)
    return dot(rows, chosen).astype(bf16)


def select_all(jac, blocks, perm):
    chunks = BS // CHUNK
    rows = jnp.concatenate(
        [
            jnp.concatenate([jac[c * CHUNK + o] for c in range(chunks)], axis=0)
            for o in range(CHUNK)
        ],
        axis=1,
    )
    picked = dot(rows, selector(blocks, COL)).astype(bf16)
    side = jnp.concatenate([picked[c * BS : (c + 1) * BS] for c in range(chunks)], axis=1)
    return dot(side, perm).astype(bf16)


def slots_of():
    return lax.broadcasted_iota(jnp.int32, (1, COL), 1) // CHUNK


def block_at(z, y, x):
    return z * 16 + y * 4 + x


def edge_kernel(forcing, jac, near, far, ends, local, sems):
    _, yg, xg = box_of(lax.axis_index("tm"))
    near_layer = jnp.where(lax.axis_index("space") % 2 == 0, LAYERS - 1, 0)
    copies = [
        pltpu.make_async_copy(
            forcing.at[:, pl.ds(pl.multiple_of(layer * LAYER, LAYER), LAYER)],
            ends.at[which],
            sems.at[which],
        )
        for which, layer in enumerate((near_layer, LAYERS - 1 - near_layer))
    ]
    copies.append(pltpu.make_async_copy(jac, local, sems.at[2]))
    for copy in copies:
        copy.start()
    scale = jnp.concatenate([scales()] * (LAYER // COL), axis=1)
    slot = slots_of()
    layer = jnp.where(slot < 4, near_layer, LAYERS - 1 - near_layer)
    blocks = block_at(layer, 2 * yg + slot // 2 % 2, 2 * xg + slot % 2)
    perm = reorder(4 * COL)
    for which, out in enumerate((near, far)):
        copies[which].wait()
        out[:STEPS] = (ends[which] * scale).astype(bf16)
    copies[2].wait()
    picked = select_all(local, blocks, perm)
    for a in range(BS // STEPS):
        cut = slice(a * 2 * COL, (a + 1) * 2 * COL)
        near[STEPS:, cut] = picked[a * STEPS : (a + 1) * STEPS, : 2 * COL]
        far[STEPS:, cut] = picked[a * STEPS : (a + 1) * STEPS, 2 * COL :]


def edges(forcing, jac):
    edge = jax.ShapeDtypeStruct((2 * STEPS, LAYER), bf16)
    hbm = pl.BlockSpec(memory_space=pltpu.HBM)
    return pl.pallas_call(
        edge_kernel,
        in_specs=[hbm, hbm],
        out_shape=(edge, edge),
        scratch_shapes=[
            pltpu.VMEM((2, STEPS, LAYER), f32),
            pltpu.VMEM((BS, BS, BLOCKS), bf16),
            pltpu.SemaphoreType.DMA((3,)),
        ],
        name="edges",
        compiler_params=pltpu.CompilerParams(vmem_limit_bytes=63 * 10**6),
        cost_estimate=cost(10**8, 2 * 10**6),
    )(forcing, jac)


def jac_kernel(jac, near, far, box, local, sem):
    copy = pltpu.make_async_copy(jac, local, sem)
    copy.start()
    zg, yg, xg = box_of(lax.axis_index("tm"))
    slot = slots_of()
    d = slot // 2 % 2
    e = slot % 2
    first = slot < 4
    own = block_at(2 * zg + slot // 4, 2 * yg + d, 2 * xg + e)
    layer = jnp.where(
        first, jnp.maximum(2 * zg - 1, 0), jnp.minimum(2 * zg + 2, LAYERS - 1)
    )
    faces = block_at(layer, 2 * yg + d, 2 * xg + e)
    beside = block_at(2 * zg + d, 2 - yg, 2 * xg + e)
    ahead = block_at(2 * zg + d, 2 * yg + e, 2 - xg)
    perm = reorder(4 * COL)
    copy.wait()
    even = lax.axis_index("space") % 2 == 0

    def other(edge):
        pieces = [edge[STEPS:, 2 * a * COL : 2 * (a + 1) * COL] for a in range(BS // STEPS)]
        return jnp.concatenate(pieces, axis=0)

    near, far = other(near), other(far)
    for at, blocks in enumerate((own, faces, jnp.where(first, beside, ahead))):
        both = select_all(local, blocks, perm)
        for which in range(2):
            value = both[:, which * 2 * COL : (which + 1) * 2 * COL]
            if at == 1 and which == 0:
                value = jnp.where(zg == 0, jnp.where(even, far, near), value)
            if at == 1 and which == 1:
                value = jnp.where(zg == 3, jnp.where(even, near, far), value)
            p = 2 * at + which
            box[:, 2 * p * COL : 2 * (p + 1) * COL] = value


def select_jac(jac, near, far):
    vmem = pl.BlockSpec(memory_space=pltpu.VMEM)
    return pl.pallas_call(
        jac_kernel,
        in_specs=[pl.BlockSpec(memory_space=pltpu.HBM), vmem, vmem],
        out_shape=jax.ShapeDtypeStruct((BS, BOX), bf16),
        scratch_shapes=[pltpu.VMEM((BS, BS, BLOCKS), bf16), pltpu.SemaphoreType.DMA],
        name="select_jac",
        compiler_params=pltpu.CompilerParams(vmem_limit_bytes=8 * 2**20),
        cost_estimate=cost(10**9, 2 * 10**6),
    )(jac, near, far)


def ops_kernel(main, mass, out, chosen, picked):
    step = pl.program_id(0)
    zg, yg, xg = box_of(lax.axis_index("tm"))

    @pl.when(step == 0)
    def _():
        slot = slots_of()
        blocks = block_at(2 * zg + slot // 4, 2 * yg + slot // 2 % 2, 2 * xg + slot % 2)
        chosen[...] = selector(blocks, COL)

    for which, source in enumerate((main, mass)):
        picked[which, step] = select_chunk(lambda o: source[o], chosen[...])

    @pl.when(step == BS // CHUNK - 1)
    def _():
        perm = reorder(4 * COL)
        both = [
            dot(
                jnp.concatenate([picked[which, c] for c in range(BS // CHUNK)], axis=1), perm
            )
            for which in range(2)
        ]
        lane = lax.broadcasted_iota(jnp.int32, (BS, 2 * COL), 1)
        low = lane % COL < BS
        zero = jnp.zeros((BS, 2 * COL), f32)
        for dz in range(2):
            for dy in range(2):
                pair = 2 * dz + dy
                cut = slice(pair * COL, (pair + 1) * COL)
                slots = [
                    jnp.concatenate([b[s * BS : (s + 1) * BS, cut] for b in both], axis=1)
                    for s in range(SLOTS)
                ]

                def put(at, value):
                    out[pair, at * BS : (at + 1) * BS] = value.astype(bf16)

                def diagonal(at, value):
                    put(at, jnp.where(low, value, zero))
                    put(at + 1, jnp.where(low, zero, value))

                put(0, jnp.where(low, slots[0], slots[1]))
                put(1, jnp.where(low, slots[2], slots[0]))
                diagonal(2, slots[6 - dz])
                diagonal(4, slots[4 - dy])
                diagonal(6, slots[5 + dz])
                faces = (yg == 1) if dy == 0 else (yg == 0)
                diagonal(8, slots[3 + dy] * jnp.where(faces, 1.0, 0.0))
                after = jnp.where(xg == 0, 1.0, 0.0)
                put(
                    10 + dy,
                    jnp.where(low, slots[1] * (1.0 - after), slots[2] * after),
                )
                put(11 - dy, zero)


def select_ops(main, mass):
    spec = pl.BlockSpec((CHUNK, SLOTS * BS, BLOCKS), lambda c: (c, 0, 0))
    return pl.pallas_call(
        ops_kernel,
        grid=(BS // CHUNK,),
        in_specs=[spec, spec],
        out_specs=pl.BlockSpec((4, 6 * COL, 2 * COL), lambda c: (0, 0, 0)),
        out_shape=jax.ShapeDtypeStruct((4, 6 * COL, 2 * COL), bf16),
        scratch_shapes=[
            pltpu.VMEM((CHUNK * BLOCKS, COL), bf16),
            pltpu.VMEM((2, BS // CHUNK, SLOTS * BS, COL), bf16),
        ],
        name="select_ops",
        compiler_params=pltpu.CompilerParams(vmem_limit_bytes=52 * 2**20),
        cost_estimate=cost(4 * 10**9, 16 * 10**6),
    )(main, mass)


def solve_kernel(recv, ops, box, table, out):
    lane = lax.broadcasted_iota(jnp.int32, (BS, 2 * COL), 1) // BS

    def diagonal(p):
        value = box[:, 2 * p * COL : 2 * (p + 1) * COL]
        rows = [jnp.where(lane == q, value, jnp.zeros_like(value)) for q in range(4)]
        return jnp.concatenate(rows, axis=0)

    diagonals = [diagonal(p) for p in range(6)]

    def fields(c, count):
        return recv[:, c * COL : (c + count) * COL]

    firsts = [dot(fields(2 * p, 2), diagonals[p]) for p in range(2)]
    halves = [value.astype(bf16) for value in firsts]
    halves += [dot(fields(2 * p, 2), diagonals[p]).astype(bf16) for p in range(2, 6)]
    lows = [half[:, e * COL : (e + 1) * COL] for half in halves for e in range(2)]

    ids = step_ids(0, LENGTH, 2 * COL).astype(f32)
    growth = jnp.exp(ids * -LOG_STEP)
    seconds = []
    for dz in range(2):
        residues = []
        for dy in range(2):
            pair = 2 * dz + dy
            around = jnp.concatenate(
                [
                    lows[pair],
                    lows[2 - 2 * dz + dy],
                    lows[2 * dz + 1 - dy],
                    lows[4 + 2 * dz + dy],
                    lows[8 + dz],
                    lows[10 + dz],
                ],
                axis=1,
            )
            image = dot(around, ops[pair])
            earlier = pltpu.roll(image[:, COL:], 1, 0)
            residue = fields(pair, 1).astype(f32) - image[:, :COL] + MODULUS * earlier
            residues.append(residue.astype(bf16))
        second = firsts[dz] + dot(jnp.concatenate(residues, axis=1), diagonals[dz])
        in_time = (second * growth).astype(bf16)
        for dest in range(PARTS):
            out[dest, 2 * STEPS :, 2 * dz * COL : 2 * (dz + 1) * COL] = in_time[
                dest * STEPS : (dest + 1) * STEPS
            ]
        seconds.append(second)
    second = jnp.concatenate(seconds, axis=1)
    high = second.astype(bf16)
    rest = (second - high.astype(f32)).astype(bf16)
    spectrum = dot(table[...], jnp.concatenate([high, rest, high], axis=0)).astype(bf16)
    for dest in range(PARTS):
        out[dest, : 2 * STEPS] = spectrum[dest * 2 * STEPS : (dest + 1) * 2 * STEPS]


def solve(recv, ops, box):
    return pl.pallas_call(
        solve_kernel,
        out_shape=jax.ShapeDtypeStruct((PARTS, 3 * STEPS, OWN), bf16),
        name="solve",
        compiler_params=pltpu.CompilerParams(vmem_limit_bytes=16 * 2**20),
        cost_estimate=cost(3 * 10**9, 5 * 10**6),
    )(recv, ops, box, jnp.asarray(dft_table()))


def unpack_kernel(recv, real, imag, in_time, ready, sems):
    copies = []
    for zg in range(4):
        for which, out in enumerate((real, imag, in_time)):
            for d in range(2):
                for rest in range(4):
                    source = 4 * zg + rest
                    _, yg, xg = box_of(source)
                    for e in range(2):
                        at = (2 * zg + d) * LAYER + (2 * yg + e) * ROW + xg * COL
                        c = 2 * d + e
                        ready[which, :, at : at + COL] = recv[
                            source,
                            which * STEPS : (which + 1) * STEPS,
                            c * COL : (c + 1) * COL,
                        ].astype(f32)
            cut = pl.ds(2 * zg * LAYER, 2 * LAYER)
            copy = pltpu.make_async_copy(
                ready.at[which, :, cut], out.at[:, cut], sems.at[len(copies)]
            )
            copy.start()
            copies.append(copy)
    for copy in copies:
        copy.wait()


def unpack(recv):
    out = jax.ShapeDtypeStruct((STEPS, SLAB), f32)
    return pl.pallas_call(
        unpack_kernel,
        out_shape=(out, out, out),
        out_specs=(pl.BlockSpec(memory_space=pltpu.HBM),) * 3,
        scratch_shapes=[pltpu.VMEM((3, STEPS, SLAB), f32), pltpu.SemaphoreType.DMA((12,))],
        name="unpack",
        compiler_params=pltpu.CompilerParams(vmem_limit_bytes=6 * 2**20),
        cost_estimate=cost(10**6, 3 * 10**6),
    )(recv)


def per_device(forcing, op_main, op_mass, jacobi_inv):
    count = lax.axis_size("space")
    across = [(i, i + 1) for i in range(1, count - 1, 2)]
    within = [(i, i + 1) for i in range(0, count, 2)]
    across += [(j, i) for i, j in across]
    within += [(j, i) for i, j in within]
    jac = jnp.transpose(jacobi_inv, (1, 2, 0))
    near, far = edges(forcing, jac)
    far = lax.ppermute(far, "space", across)
    near = lax.ppermute(near, "space", within)
    packed = pack(forcing)
    near, far, packed = lax.optimization_barrier((near, far, packed))
    packed = patch(packed, near, far)
    packed, op_main, op_mass = lax.optimization_barrier((packed, op_main, op_mass))
    recv = lax.all_to_all(packed, "tm", 0, 0).reshape(LENGTH, BOX)
    ops = select_ops(jnp.transpose(op_main, (1, 2, 0)), jnp.transpose(op_mass, (1, 2, 0)))
    ops, jac = lax.optimization_barrier((ops, jac))
    box = select_jac(jac, near, far)
    sent = solve(recv, ops, box)
    back = lax.all_to_all(sent, "tm", 0, 0)
    return unpack(back)


def solution(mesh):
    in_specs = (
        P("tm", "space"),
        P("space", None, None),
        P("space", None, None),
        P("space", None, None),
    )
    out_specs = (P("tm", "space"), P("tm", "space"), P("tm", "space"))
    return jax.shard_map(
        per_device, mesh=mesh, in_specs=in_specs, out_specs=out_specs, check_vma=False
    )
```

```python
import functools
import math

import jax
import jax.numpy as jnp
import ml_dtypes
import numpy as np
from jax import lax
from jax.experimental import pallas as pl
from jax.experimental.pallas import tpu as pltpu
from jax.sharding import PartitionSpec as P

LENGTH = 256
PARTS = 16
STEPS = LENGTH // PARTS
BS = 64
LAYER = 1024
ROW = 256
LAYERS = 8
SLAB = LAYERS * LAYER
BLOCKS = SLAB // BS
SLOTS = 7
COL = 128
OWN = 4 * COL
BOX = 12 * COL
CHUNK = 16

ALPHA = 0.25
LOG_STEP = math.log(ALPHA) / LENGTH
MODULUS = ALPHA ** (1.0 / LENGTH)

f32 = jnp.float32
bf16 = jnp.bfloat16


def box_of(part):
    return part // 4, part // 2 % 2, part % 2


def dft_table():
    freq = np.arange(LENGTH)[:, None]
    step = np.arange(LENGTH)[None, :]
    angle = 2.0 * np.pi * (freq * step % LENGTH) / LENGTH
    table = np.stack([np.cos(angle), -np.sin(angle)], 1) / math.sqrt(LENGTH)
    table = table.reshape(PARTS, STEPS, 2, LENGTH).transpose(0, 2, 1, 3)
    table = table.reshape(2 * LENGTH, LENGTH)
    high = table.astype(ml_dtypes.bfloat16)
    low = (table - high.astype(np.float64)).astype(ml_dtypes.bfloat16)
    return np.concatenate([high, high, low], axis=1)


def step_ids(part, count, width):
    return part * STEPS + lax.broadcasted_iota(jnp.int32, (count, width), 0)


def cost(flops, nbytes):
    return pl.CostEstimate(flops=flops, bytes_accessed=nbytes, transcendentals=0)


def dot(a, b):
    return jnp.dot(a, b, preferred_element_type=f32)


def scales():
    ids = step_ids(lax.axis_index("tm"), STEPS, COL).astype(f32)
    return jnp.exp(ids * LOG_STEP)


def pack_kernel(forcing, out):
    scale = scales()
    half = lax.broadcasted_iota(jnp.int32, (STEPS, COL), 1) < BS

    def column(z, y, x):
        at = z * LAYER + y * ROW + x * COL
        return forcing[:, at : at + COL] * scale

    def put(dest, c, value):
        out[dest, :, c * COL : (c + 1) * COL] = value.astype(bf16)

    for dest in range(PARTS):
        zg, yg, xg = box_of(dest)
        for d in range(2):
            for e in range(2):
                put(dest, 2 * d + e, column(2 * zg + d, 2 * yg + e, xg))
            y = 2 * yg + d
            if zg > 0:
                put(dest, 4 + d, column(2 * zg - 1, y, xg))
            if zg < 3:
                put(dest, 6 + d, column(2 * zg + 2, y, xg))
            z = 2 * zg + d
            put(dest, 8 + d, column(z, 2 - yg, xg))
            first = column(z, 2 * yg, 1 - xg)
            second = column(z, 2 * yg + 1, 1 - xg)
            if xg == 0:
                pair = jnp.where(half, first, pltpu.roll(second, BS, 1))
            else:
                pair = jnp.where(half, pltpu.roll(first, BS, 1), second)
            put(dest, 10 + d, pair)


def pack(forcing):
    return pl.pallas_call(
        pack_kernel,
        in_specs=[pl.BlockSpec(memory_space=pltpu.VMEM)],
        out_shape=jax.ShapeDtypeStruct((PARTS, STEPS, BOX), bf16),
        name="pack",
        compiler_params=pltpu.CompilerParams(vmem_limit_bytes=6 * 2**20),
        cost_estimate=cost(10**6, 4 * 10**6),
    )(forcing)


def patch_kernel(packed, far, near, out, sems):
    def place(low_edge, high_edge):
        copies = []
        for dest in range(PARTS):
            zg, yg, xg = box_of(dest)
            for edge, at_group, first in ((low_edge, 0, 4), (high_edge, 3, 6)):
                if zg == at_group:
                    for d in range(2):
                        at = (2 * yg + d) * ROW + xg * COL
                        copies.append(
                            pltpu.make_async_copy(
                                edge.at[pl.ds(0, STEPS), pl.ds(at, COL)],
                                out.at[dest, :, pl.ds((first + d) * COL, COL)],
                                sems.at[len(copies)],
                            )
                        )
        for copy in copies:
            copy.start()
        for copy in copies:
            copy.wait()

    core = lax.axis_index("space") % 2

    @pl.when(core == 0)
    def _():
        place(far, near)

    @pl.when(core == 1)
    def _():
        place(near, far)


def patch(packed, far, near):
    anywhere = pl.BlockSpec(memory_space=pl.ANY)
    return pl.pallas_call(
        patch_kernel,
        in_specs=[anywhere] * 3,
        out_specs=anywhere,
        out_shape=jax.ShapeDtypeStruct((PARTS, STEPS, BOX), bf16),
        scratch_shapes=[pltpu.SemaphoreType.DMA((16,))],
        input_output_aliases={0: 0},
        name="patch",
        compiler_params=pltpu.CompilerParams(vmem_limit_bytes=2**20),
        cost_estimate=cost(10**3, 2 * 10**5),
    )(packed, far, near)


def selector(blocks, width):
    block = lax.broadcasted_iota(jnp.int32, (BLOCKS, width), 0)
    lane = lax.broadcasted_iota(jnp.int32, (BLOCKS, width), 1)
    hit = block == blocks
    pieces = [
        jnp.where(hit & (lane % CHUNK == o), 1.0, 0.0).astype(bf16) for o in range(CHUNK)
    ]
    return jnp.concatenate(pieces, axis=0)


def reorder(width):
    slots = width // BS
    source = lax.broadcasted_iota(jnp.int32, (width, width), 0)
    lane = lax.broadcasted_iota(jnp.int32, (width, width), 1)
    wanted = lane % BS // CHUNK * (slots * CHUNK) + lane // BS * CHUNK + lane % CHUNK
    return jnp.where(source == wanted, 1.0, 0.0).astype(bf16)


def select_chunk(read, chosen):
    rows = jnp.concatenate([read(o) for o in range(CHUNK)], axis=1)
    return dot(rows, chosen).astype(bf16)


def select_all(jac, blocks, perm):
    chunks = BS // CHUNK
    rows = jnp.concatenate(
        [
            jnp.concatenate([jac[c * CHUNK + o] for c in range(chunks)], axis=0)
            for o in range(CHUNK)
        ],
        axis=1,
    )
    picked = dot(rows, selector(blocks, COL)).astype(bf16)
    side = jnp.concatenate([picked[c * BS : (c + 1) * BS] for c in range(chunks)], axis=1)
    return dot(side, perm).astype(bf16)


def slots_of():
    return lax.broadcasted_iota(jnp.int32, (1, COL), 1) // CHUNK


def block_at(z, y, x):
    return z * 16 + y * 4 + x


def edge_kernel(forcing, jac, far, near, held, local, sems):
    _, yg, xg = box_of(lax.axis_index("tm"))
    near_layer = jnp.where(lax.axis_index("space") % 2 == 0, LAYERS - 1, 0)
    first, middle, last = LAYER, SLAB - 2 * LAYER, LAYER
    cuts = [pl.ds(0, first), pl.ds(SLAB - last, last), pl.ds(first, middle)]
    copies = [
        pltpu.make_async_copy(forcing.at[:, cut], held.at[:, cut], sems.at[which])
        for which, cut in enumerate(cuts)
    ]
    copies.append(pltpu.make_async_copy(jac, local, sems.at[3]))
    for which in (0, 1, 3, 2):
        copies[which].start()
    scale = jnp.concatenate([scales()] * (LAYER // COL), axis=1)
    slot = slots_of()
    layer = jnp.where(slot < 4, near_layer, LAYERS - 1 - near_layer)
    blocks = block_at(layer, 2 * yg + slot // 2 % 2, 2 * xg + slot % 2)
    perm = reorder(4 * COL)
    copies[0].wait()
    copies[1].wait()
    bottom = (held[:, :LAYER] * scale).astype(bf16)
    top = (held[:, SLAB - LAYER :] * scale).astype(bf16)
    even = near_layer > 0
    near[:STEPS] = jnp.where(even, top, bottom)
    far[:STEPS] = jnp.where(even, bottom, top)
    copies[3].wait()
    picked = select_all(local, blocks, perm)
    for a in range(BS // STEPS):
        cut = slice(a * 2 * COL, (a + 1) * 2 * COL)
        near[STEPS:, cut] = picked[a * STEPS : (a + 1) * STEPS, : 2 * COL]
        far[STEPS:, cut] = picked[a * STEPS : (a + 1) * STEPS, 2 * COL :]
    copies[2].wait()


def edges(forcing, jac):
    edge = jax.ShapeDtypeStruct((2 * STEPS, LAYER), bf16)
    hbm = pl.BlockSpec(memory_space=pltpu.HBM)
    return pl.pallas_call(
        edge_kernel,
        in_specs=[hbm, hbm],
        out_shape=(edge, edge, jax.ShapeDtypeStruct((STEPS, SLAB), f32)),
        scratch_shapes=[
            pltpu.VMEM((BS, BS, BLOCKS), bf16),
            pltpu.SemaphoreType.DMA((4,)),
        ],
        name="edges",
        compiler_params=pltpu.CompilerParams(vmem_limit_bytes=6 * 2**20),
        cost_estimate=cost(10**8, 2 * 10**6),
    )(forcing, jac)


def jac_kernel(jac, far, near, box, local, sem):
    copy = pltpu.make_async_copy(jac, local, sem)
    copy.start()
    zg, yg, xg = box_of(lax.axis_index("tm"))
    slot = slots_of()
    d = slot // 2 % 2
    e = slot % 2
    first = slot < 4
    own = block_at(2 * zg + slot // 4, 2 * yg + d, 2 * xg + e)
    layer = jnp.where(
        first, jnp.maximum(2 * zg - 1, 0), jnp.minimum(2 * zg + 2, LAYERS - 1)
    )
    faces = block_at(layer, 2 * yg + d, 2 * xg + e)
    beside = block_at(2 * zg + d, 2 - yg, 2 * xg + e)
    ahead = block_at(2 * zg + d, 2 * yg + e, 2 - xg)
    perm = reorder(4 * COL)
    copy.wait()
    even = lax.axis_index("space") % 2 == 0

    def other(edge):
        pieces = [edge[STEPS:, 2 * a * COL : 2 * (a + 1) * COL] for a in range(BS // STEPS)]
        return jnp.concatenate(pieces, axis=0)

    near, far = other(near), other(far)
    for at, blocks in enumerate((own, faces, jnp.where(first, beside, ahead))):
        both = select_all(local, blocks, perm)
        for which in range(2):
            value = both[:, which * 2 * COL : (which + 1) * 2 * COL]
            if at == 1 and which == 0:
                value = jnp.where(zg == 0, jnp.where(even, far, near), value)
            if at == 1 and which == 1:
                value = jnp.where(zg == 3, jnp.where(even, near, far), value)
            p = 2 * at + which
            box[:, 2 * p * COL : 2 * (p + 1) * COL] = value


def select_jac(jac, far, near):
    vmem = pl.BlockSpec(memory_space=pltpu.VMEM)
    return pl.pallas_call(
        jac_kernel,
        in_specs=[pl.BlockSpec(memory_space=pltpu.HBM), vmem, vmem],
        out_shape=jax.ShapeDtypeStruct((BS, BOX), bf16),
        scratch_shapes=[pltpu.VMEM((BS, BS, BLOCKS), bf16), pltpu.SemaphoreType.DMA],
        name="select_jac",
        compiler_params=pltpu.CompilerParams(vmem_limit_bytes=8 * 2**20),
        cost_estimate=cost(10**9, 2 * 10**6),
    )(jac, far, near)


def ops_kernel(main, mass, out, chosen, picked):
    step = pl.program_id(0)
    zg, yg, xg = box_of(lax.axis_index("tm"))

    @pl.when(step == 0)
    def _():
        slot = slots_of()
        blocks = block_at(2 * zg + slot // 4, 2 * yg + slot // 2 % 2, 2 * xg + slot % 2)
        chosen[...] = selector(blocks, COL)

    for which, source in enumerate((main, mass)):
        picked[which, step] = select_chunk(lambda o: source[o], chosen[...])

    @pl.when(step == BS // CHUNK - 1)
    def _():
        perm = reorder(4 * COL)
        both = [
            dot(
                jnp.concatenate([picked[which, c] for c in range(BS // CHUNK)], axis=1), perm
            )
            for which in range(2)
        ]
        lane = lax.broadcasted_iota(jnp.int32, (BS, 2 * COL), 1)
        low = lane % COL < BS
        zero = jnp.zeros((BS, 2 * COL), f32)
        for dz in range(2):
            for dy in range(2):
                pair = 2 * dz + dy
                cut = slice(pair * COL, (pair + 1) * COL)
                slots = [
                    jnp.concatenate([b[s * BS : (s + 1) * BS, cut] for b in both], axis=1)
                    for s in range(SLOTS)
                ]

                def put(at, value):
                    out[pair, at * BS : (at + 1) * BS] = value.astype(bf16)

                def diagonal(at, value):
                    put(at, jnp.where(low, value, zero))
                    put(at + 1, jnp.where(low, zero, value))

                put(0, jnp.where(low, slots[0], slots[1]))
                put(1, jnp.where(low, slots[2], slots[0]))
                diagonal(2, slots[6 - dz])
                diagonal(4, slots[4 - dy])
                diagonal(6, slots[5 + dz])
                faces = (yg == 1) if dy == 0 else (yg == 0)
                diagonal(8, slots[3 + dy] * jnp.where(faces, 1.0, 0.0))
                after = jnp.where(xg == 0, 1.0, 0.0)
                put(
                    10 + dy,
                    jnp.where(low, slots[1] * (1.0 - after), slots[2] * after),
                )
                put(11 - dy, zero)


def select_ops(main, mass):
    spec = pl.BlockSpec((CHUNK, SLOTS * BS, BLOCKS), lambda c: (c, 0, 0))
    return pl.pallas_call(
        ops_kernel,
        grid=(BS // CHUNK,),
        in_specs=[spec, spec],
        out_specs=pl.BlockSpec((4, 6 * COL, 2 * COL), lambda c: (0, 0, 0)),
        out_shape=jax.ShapeDtypeStruct((4, 6 * COL, 2 * COL), bf16),
        scratch_shapes=[
            pltpu.VMEM((CHUNK * BLOCKS, COL), bf16),
            pltpu.VMEM((2, BS // CHUNK, SLOTS * BS, COL), bf16),
        ],
        name="select_ops",
        compiler_params=pltpu.CompilerParams(vmem_limit_bytes=52 * 2**20),
        cost_estimate=cost(4 * 10**9, 16 * 10**6),
    )(main, mass)


def solve_kernel(recv, ops, box, table, out):
    lane = lax.broadcasted_iota(jnp.int32, (BS, 2 * COL), 1) // BS

    def diagonal(p):
        value = box[:, 2 * p * COL : 2 * (p + 1) * COL]
        rows = [jnp.where(lane == q, value, jnp.zeros_like(value)) for q in range(4)]
        return jnp.concatenate(rows, axis=0)

    diagonals = [diagonal(p) for p in range(6)]

    def fields(c, count):
        return recv[:, c * COL : (c + count) * COL]

    firsts = [dot(fields(2 * p, 2), diagonals[p]) for p in range(2)]
    halves = [value.astype(bf16) for value in firsts]
    halves += [dot(fields(2 * p, 2), diagonals[p]).astype(bf16) for p in range(2, 6)]
    lows = [half[:, e * COL : (e + 1) * COL] for half in halves for e in range(2)]

    ids = step_ids(0, LENGTH, 2 * COL).astype(f32)
    growth = jnp.exp(ids * -LOG_STEP)
    seconds = []
    for dz in range(2):
        residues = []
        for dy in range(2):
            pair = 2 * dz + dy
            around = jnp.concatenate(
                [
                    lows[pair],
                    lows[2 - 2 * dz + dy],
                    lows[2 * dz + 1 - dy],
                    lows[4 + 2 * dz + dy],
                    lows[8 + dz],
                    lows[10 + dz],
                ],
                axis=1,
            )
            image = dot(around, ops[pair])
            earlier = pltpu.roll(image[:, COL:], 1, 0)
            residue = fields(pair, 1).astype(f32) - image[:, :COL] + MODULUS * earlier
            residues.append(residue.astype(bf16))
        second = firsts[dz] + dot(jnp.concatenate(residues, axis=1), diagonals[dz])
        in_time = (second * growth).astype(bf16)
        for dest in range(PARTS):
            out[dest, 2 * STEPS :, 2 * dz * COL : 2 * (dz + 1) * COL] = in_time[
                dest * STEPS : (dest + 1) * STEPS
            ]
        seconds.append(second)
    second = jnp.concatenate(seconds, axis=1)
    high = second.astype(bf16)
    rest = (second - high.astype(f32)).astype(bf16)
    spectrum = dot(table[...], jnp.concatenate([high, rest, high], axis=0)).astype(bf16)
    for dest in range(PARTS):
        out[dest, : 2 * STEPS] = spectrum[dest * 2 * STEPS : (dest + 1) * 2 * STEPS]


def solve(recv, ops, box):
    return pl.pallas_call(
        solve_kernel,
        out_shape=jax.ShapeDtypeStruct((PARTS, 3 * STEPS, OWN), bf16),
        name="solve",
        compiler_params=pltpu.CompilerParams(vmem_limit_bytes=16 * 2**20),
        cost_estimate=cost(3 * 10**9, 5 * 10**6),
    )(recv, ops, box, jnp.asarray(dft_table()))


def unpack_kernel(recv, real, imag, in_time, ready, sems):
    copies = []
    for zg in range(4):
        for which, out in enumerate((real, imag, in_time)):
            for d in range(2):
                for rest in range(4):
                    source = 4 * zg + rest
                    _, yg, xg = box_of(source)
                    for e in range(2):
                        at = (2 * zg + d) * LAYER + (2 * yg + e) * ROW + xg * COL
                        c = 2 * d + e
                        ready[which, :, at : at + COL] = recv[
                            source,
                            which * STEPS : (which + 1) * STEPS,
                            c * COL : (c + 1) * COL,
                        ].astype(f32)
            cut = pl.ds(2 * zg * LAYER, 2 * LAYER)
            copy = pltpu.make_async_copy(
                ready.at[which, :, cut], out.at[:, cut], sems.at[len(copies)]
            )
            copy.start()
            copies.append(copy)
    for copy in copies:
        copy.wait()


def unpack(recv):
    out = jax.ShapeDtypeStruct((STEPS, SLAB), f32)
    return pl.pallas_call(
        unpack_kernel,
        out_shape=(out, out, out),
        out_specs=(pl.BlockSpec(memory_space=pltpu.HBM),) * 3,
        scratch_shapes=[pltpu.VMEM((3, STEPS, SLAB), f32), pltpu.SemaphoreType.DMA((12,))],
        name="unpack",
        compiler_params=pltpu.CompilerParams(vmem_limit_bytes=6 * 2**20),
        cost_estimate=cost(10**6, 3 * 10**6),
    )(recv)


def per_device(forcing, op_main, op_mass, jacobi_inv):
    count = lax.axis_size("space")
    across = [(i, i + 1) for i in range(1, count - 1, 2)]
    within = [(i, i + 1) for i in range(0, count, 2)]
    across += [(j, i) for i, j in across]
    within += [(j, i) for i, j in within]
    jac = jnp.transpose(jacobi_inv, (1, 2, 0))
    forcing = pltpu.with_memory_space_constraint(forcing, pltpu.HBM)
    far, near, held = edges(forcing, pltpu.with_memory_space_constraint(jac, pltpu.HBM))
    far = lax.ppermute(far, "space", across)
    near = lax.ppermute(near, "space", within)
    packed = pack(pltpu.with_memory_space_constraint(held, pltpu.VMEM))
    far, near, packed = lax.optimization_barrier((far, near, packed))
    packed = patch(packed, far, near)
    packed, op_main, op_mass = lax.optimization_barrier((packed, op_main, op_mass))
    recv = lax.all_to_all(packed, "tm", 0, 0).reshape(LENGTH, BOX)
    ops = select_ops(jnp.transpose(op_main, (1, 2, 0)), jnp.transpose(op_mass, (1, 2, 0)))
    ops, jac = lax.optimization_barrier((ops, jac))
    box = select_jac(jac, far, near)
    sent = solve(recv, ops, box)
    back = lax.all_to_all(sent, "tm", 0, 0)
    return unpack(back)


def solution(mesh):
    in_specs = (
        P("tm", "space"),
        P("space", None, None),
        P("space", None, None),
        P("space", None, None),
    )
    out_specs = (P("tm", "space"), P("tm", "space"), P("tm", "space"))
    return jax.shard_map(
        per_device, mesh=mesh, in_specs=in_specs, out_specs=out_specs, check_vma=False
    )
```

```python
import functools
import math

import jax
import jax.numpy as jnp
import ml_dtypes
import numpy as np
from jax import lax
from jax.experimental import pallas as pl
from jax.experimental.pallas import tpu as pltpu
from jax.sharding import PartitionSpec as P

LENGTH = 256
PARTS = 16
STEPS = LENGTH // PARTS
BS = 64
LAYER = 1024
ROW = 256
LAYERS = 8
SLAB = LAYERS * LAYER
BLOCKS = SLAB // BS
SLOTS = 7
COL = 128
OWN = 4 * COL
BOX = 12 * COL
CHUNK = 16

ALPHA = 0.25
LOG_STEP = math.log(ALPHA) / LENGTH
MODULUS = ALPHA ** (1.0 / LENGTH)

f32 = jnp.float32
bf16 = jnp.bfloat16


def box_of(part):
    return part // 4, part // 2 % 2, part % 2


def dft_table():
    freq = np.arange(LENGTH)[:, None]
    step = np.arange(LENGTH)[None, :]
    angle = 2.0 * np.pi * (freq * step % LENGTH) / LENGTH
    table = np.stack([np.cos(angle), -np.sin(angle)], 1) / math.sqrt(LENGTH)
    table = table.reshape(PARTS, STEPS, 2, LENGTH).transpose(0, 2, 1, 3)
    table = table.reshape(2 * LENGTH, LENGTH)
    high = table.astype(ml_dtypes.bfloat16)
    low = (table - high.astype(np.float64)).astype(ml_dtypes.bfloat16)
    return np.concatenate([high, high, low], axis=1)


def step_ids(part, count, width):
    return part * STEPS + lax.broadcasted_iota(jnp.int32, (count, width), 0)


def cost(flops, nbytes):
    return pl.CostEstimate(flops=flops, bytes_accessed=nbytes, transcendentals=0)


def dot(a, b):
    return jnp.dot(a, b, preferred_element_type=f32)


def scales():
    ids = step_ids(lax.axis_index("tm"), STEPS, COL).astype(f32)
    return jnp.exp(ids * LOG_STEP)


def pack_kernel(forcing, out):
    scale = scales()
    half = lax.broadcasted_iota(jnp.int32, (STEPS, COL), 1) < BS

    def column(z, y, x):
        at = z * LAYER + y * ROW + x * COL
        return forcing[:, at : at + COL] * scale

    def put(dest, c, value):
        out[dest, :, c * COL : (c + 1) * COL] = value.astype(bf16)

    for dest in range(PARTS):
        zg, yg, xg = box_of(dest)
        for d in range(2):
            for e in range(2):
                put(dest, 2 * d + e, column(2 * zg + d, 2 * yg + e, xg))
            y = 2 * yg + d
            if zg > 0:
                put(dest, 4 + d, column(2 * zg - 1, y, xg))
            if zg < 3:
                put(dest, 6 + d, column(2 * zg + 2, y, xg))
            z = 2 * zg + d
            put(dest, 8 + d, column(z, 2 - yg, xg))
            first = column(z, 2 * yg, 1 - xg)
            second = column(z, 2 * yg + 1, 1 - xg)
            if xg == 0:
                pair = jnp.where(half, first, pltpu.roll(second, BS, 1))
            else:
                pair = jnp.where(half, pltpu.roll(first, BS, 1), second)
            put(dest, 10 + d, pair)


def pack(forcing):
    return pl.pallas_call(
        pack_kernel,
        in_specs=[pl.BlockSpec(memory_space=pltpu.VMEM)],
        out_shape=jax.ShapeDtypeStruct((PARTS, STEPS, BOX), bf16),
        name="pack",
        compiler_params=pltpu.CompilerParams(vmem_limit_bytes=6 * 2**20),
        cost_estimate=cost(10**6, 4 * 10**6),
    )(forcing)


def patch_kernel(packed, far, near, out, sems):
    def place(low_edge, high_edge):
        copies = []
        for dest in range(PARTS):
            zg, yg, xg = box_of(dest)
            for edge, at_group, first in ((low_edge, 0, 4), (high_edge, 3, 6)):
                if zg == at_group:
                    at = (2 * yg + xg) * 2 * COL
                    copies.append(
                        pltpu.make_async_copy(
                            edge.at[pl.ds(0, STEPS), pl.ds(at, 2 * COL)],
                            out.at[dest, :, pl.ds(first * COL, 2 * COL)],
                            sems.at[len(copies)],
                        )
                    )
        for copy in copies:
            copy.start()
        for copy in copies:
            copy.wait()

    core = lax.axis_index("space") % 2

    @pl.when(core == 0)
    def _():
        place(far, near)

    @pl.when(core == 1)
    def _():
        place(near, far)


def patch(packed, far, near):
    anywhere = pl.BlockSpec(memory_space=pl.ANY)
    return pl.pallas_call(
        patch_kernel,
        in_specs=[anywhere] * 3,
        out_specs=anywhere,
        out_shape=jax.ShapeDtypeStruct((PARTS, STEPS, BOX), bf16),
        scratch_shapes=[pltpu.SemaphoreType.DMA((8,))],
        input_output_aliases={0: 0},
        name="patch",
        compiler_params=pltpu.CompilerParams(vmem_limit_bytes=2**20),
        cost_estimate=cost(10**3, 2 * 10**5),
    )(packed, far, near)


def selector(blocks, width):
    block = lax.broadcasted_iota(jnp.int32, (BLOCKS, width), 0)
    lane = lax.broadcasted_iota(jnp.int32, (BLOCKS, width), 1)
    hit = block == blocks
    pieces = [
        jnp.where(hit & (lane % CHUNK == o), 1.0, 0.0).astype(bf16) for o in range(CHUNK)
    ]
    return jnp.concatenate(pieces, axis=0)


def reorder(width):
    slots = width // BS
    source = lax.broadcasted_iota(jnp.int32, (width, width), 0)
    lane = lax.broadcasted_iota(jnp.int32, (width, width), 1)
    wanted = lane % BS // CHUNK * (slots * CHUNK) + lane // BS * CHUNK + lane % CHUNK
    return jnp.where(source == wanted, 1.0, 0.0).astype(bf16)


def select_chunk(read, chosen):
    rows = jnp.concatenate([read(o) for o in range(CHUNK)], axis=1)
    return dot(rows, chosen).astype(bf16)


def select_all(jac, chosen, perm):
    chunks = BS // CHUNK
    rows = jnp.concatenate(
        [
            jnp.concatenate([jac[c * CHUNK + o] for c in range(chunks)], axis=0)
            for o in range(CHUNK)
        ],
        axis=1,
    )
    picked = dot(rows, chosen).astype(bf16)
    side = jnp.concatenate([picked[c * BS : (c + 1) * BS] for c in range(chunks)], axis=1)
    return dot(side, perm).astype(bf16)


def slots_of():
    return lax.broadcasted_iota(jnp.int32, (1, COL), 1) // CHUNK


def block_at(z, y, x):
    return z * 16 + y * 4 + x


def edge_kernel(forcing, jac, far, near, held, local, sems):
    _, yg, xg = box_of(lax.axis_index("tm"))
    near_layer = jnp.where(lax.axis_index("space") % 2 == 0, LAYERS - 1, 0)
    first, middle, last = LAYER, SLAB - 2 * LAYER, LAYER
    cuts = [pl.ds(0, first), pl.ds(SLAB - last, last), pl.ds(first, middle)]
    copies = [
        pltpu.make_async_copy(forcing.at[:, cut], held.at[:, cut], sems.at[which])
        for which, cut in enumerate(cuts)
    ]
    for c in range(BS // CHUNK):
        cut = pl.ds(c * CHUNK, CHUNK)
        copies.append(pltpu.make_async_copy(jac.at[cut], local.at[cut], sems.at[3 + c]))
    for which in (0, 1, 3, 4, 5, 6, 2):
        copies[which].start()
    scale = scales()
    slot = slots_of()
    layer = jnp.where(slot < 4, near_layer, LAYERS - 1 - near_layer)
    chosen = selector(
        block_at(layer, 2 * yg + slot // 2 % 2, 2 * xg + slot % 2), COL
    )
    perm = reorder(4 * COL)
    copies[0].wait()
    copies[1].wait()
    even = near_layer > 0
    for target in range(4):
        for d in range(2):
            at = (2 * (target // 2) + d) * ROW + target % 2 * COL
            to = slice((2 * target + d) * COL, (2 * target + d + 1) * COL)
            bottom = (held[:, at : at + COL] * scale).astype(bf16)
            at += SLAB - LAYER
            top = (held[:, at : at + COL] * scale).astype(bf16)
            near[:STEPS, to] = jnp.where(even, top, bottom)
            far[:STEPS, to] = jnp.where(even, bottom, top)
    for c in range(BS // CHUNK):
        copies[3 + c].wait()
    picked = select_all(local, chosen, perm)
    for a in range(BS // STEPS):
        cut = slice(a * 2 * COL, (a + 1) * 2 * COL)
        near[STEPS:, cut] = picked[a * STEPS : (a + 1) * STEPS, : 2 * COL]
        far[STEPS:, cut] = picked[a * STEPS : (a + 1) * STEPS, 2 * COL :]
    copies[2].wait()


def edges(forcing, jac):
    edge = jax.ShapeDtypeStruct((2 * STEPS, LAYER), bf16)
    hbm = pl.BlockSpec(memory_space=pltpu.HBM)
    return pl.pallas_call(
        edge_kernel,
        in_specs=[hbm, hbm],
        out_shape=(edge, edge, jax.ShapeDtypeStruct((STEPS, SLAB), f32)),
        scratch_shapes=[
            pltpu.VMEM((BS, BS, BLOCKS), bf16),
            pltpu.SemaphoreType.DMA((7,)),
        ],
        name="edges",
        compiler_params=pltpu.CompilerParams(vmem_limit_bytes=6 * 2**20),
        cost_estimate=cost(10**8, 2 * 10**6),
    )(forcing, jac)


def jac_kernel(jac, far, near, box, local, sem):
    copy = pltpu.make_async_copy(jac, local, sem)
    copy.start()
    zg, yg, xg = box_of(lax.axis_index("tm"))
    slot = slots_of()
    d = slot // 2 % 2
    e = slot % 2
    first = slot < 4
    own = block_at(2 * zg + slot // 4, 2 * yg + d, 2 * xg + e)
    layer = jnp.where(
        first, jnp.maximum(2 * zg - 1, 0), jnp.minimum(2 * zg + 2, LAYERS - 1)
    )
    faces = block_at(layer, 2 * yg + d, 2 * xg + e)
    beside = block_at(2 * zg + d, 2 - yg, 2 * xg + e)
    ahead = block_at(2 * zg + d, 2 * yg + e, 2 - xg)
    perm = reorder(4 * COL)
    copy.wait()
    even = lax.axis_index("space") % 2 == 0

    def other(edge):
        pieces = [edge[STEPS:, 2 * a * COL : 2 * (a + 1) * COL] for a in range(BS // STEPS)]
        return jnp.concatenate(pieces, axis=0)

    near, far = other(near), other(far)
    for at, blocks in enumerate((own, faces, jnp.where(first, beside, ahead))):
        both = select_all(local, selector(blocks, COL), perm)
        for which in range(2):
            value = both[:, which * 2 * COL : (which + 1) * 2 * COL]
            if at == 1 and which == 0:
                value = jnp.where(zg == 0, jnp.where(even, far, near), value)
            if at == 1 and which == 1:
                value = jnp.where(zg == 3, jnp.where(even, near, far), value)
            p = 2 * at + which
            box[:, 2 * p * COL : 2 * (p + 1) * COL] = value


def select_jac(jac, far, near):
    vmem = pl.BlockSpec(memory_space=pltpu.VMEM)
    return pl.pallas_call(
        jac_kernel,
        in_specs=[pl.BlockSpec(memory_space=pltpu.HBM), vmem, vmem],
        out_shape=jax.ShapeDtypeStruct((BS, BOX), bf16),
        scratch_shapes=[pltpu.VMEM((BS, BS, BLOCKS), bf16), pltpu.SemaphoreType.DMA],
        name="select_jac",
        compiler_params=pltpu.CompilerParams(vmem_limit_bytes=8 * 2**20),
        cost_estimate=cost(10**9, 2 * 10**6),
    )(jac, far, near)


def ops_kernel(main, mass, out, chosen, picked):
    step = pl.program_id(0)
    zg, yg, xg = box_of(lax.axis_index("tm"))

    @pl.when(step == 0)
    def _():
        slot = slots_of()
        blocks = block_at(2 * zg + slot // 4, 2 * yg + slot // 2 % 2, 2 * xg + slot % 2)
        chosen[...] = selector(blocks, COL)

    for which, source in enumerate((main, mass)):
        picked[which, step] = select_chunk(lambda o: source[o], chosen[...])

    @pl.when(step == BS // CHUNK - 1)
    def _():
        perm = reorder(4 * COL)
        both = [
            dot(
                jnp.concatenate([picked[which, c] for c in range(BS // CHUNK)], axis=1), perm
            )
            for which in range(2)
        ]
        lane = lax.broadcasted_iota(jnp.int32, (BS, 2 * COL), 1)
        low = lane % COL < BS
        zero = jnp.zeros((BS, 2 * COL), f32)
        for dz in range(2):
            for dy in range(2):
                pair = 2 * dz + dy
                cut = slice(pair * COL, (pair + 1) * COL)
                slots = [
                    jnp.concatenate([b[s * BS : (s + 1) * BS, cut] for b in both], axis=1)
                    for s in range(SLOTS)
                ]

                def put(at, value):
                    out[pair, at * BS : (at + 1) * BS] = value.astype(bf16)

                def diagonal(at, value):
                    put(at, jnp.where(low, value, zero))
                    put(at + 1, jnp.where(low, zero, value))

                put(0, jnp.where(low, slots[0], slots[1]))
                put(1, jnp.where(low, slots[2], slots[0]))
                diagonal(2, slots[6 - dz])
                diagonal(4, slots[4 - dy])
                diagonal(6, slots[5 + dz])
                faces = (yg == 1) if dy == 0 else (yg == 0)
                diagonal(8, slots[3 + dy] * jnp.where(faces, 1.0, 0.0))
                after = jnp.where(xg == 0, 1.0, 0.0)
                put(
                    10 + dy,
                    jnp.where(low, slots[1] * (1.0 - after), slots[2] * after),
                )
                put(11 - dy, zero)


def select_ops(main, mass):
    spec = pl.BlockSpec((CHUNK, SLOTS * BS, BLOCKS), lambda c: (c, 0, 0))
    return pl.pallas_call(
        ops_kernel,
        grid=(BS // CHUNK,),
        in_specs=[spec, spec],
        out_specs=pl.BlockSpec((4, 6 * COL, 2 * COL), lambda c: (0, 0, 0)),
        out_shape=jax.ShapeDtypeStruct((4, 6 * COL, 2 * COL), bf16),
        scratch_shapes=[
            pltpu.VMEM((CHUNK * BLOCKS, COL), bf16),
            pltpu.VMEM((2, BS // CHUNK, SLOTS * BS, COL), bf16),
        ],
        name="select_ops",
        compiler_params=pltpu.CompilerParams(vmem_limit_bytes=52 * 2**20),
        cost_estimate=cost(4 * 10**9, 16 * 10**6),
    )(main, mass)


def solve_kernel(recv, ops, box, table, out):
    lane = lax.broadcasted_iota(jnp.int32, (BS, 2 * COL), 1) // BS

    def diagonal(p):
        value = box[:, 2 * p * COL : 2 * (p + 1) * COL]
        rows = [jnp.where(lane == q, value, jnp.zeros_like(value)) for q in range(4)]
        return jnp.concatenate(rows, axis=0)

    diagonals = [diagonal(p) for p in range(6)]

    def fields(c, count):
        return recv[:, c * COL : (c + count) * COL]

    firsts = [dot(fields(2 * p, 2), diagonals[p]) for p in range(2)]
    halves = [value.astype(bf16) for value in firsts]
    halves += [dot(fields(2 * p, 2), diagonals[p]).astype(bf16) for p in range(2, 6)]
    lows = [half[:, e * COL : (e + 1) * COL] for half in halves for e in range(2)]

    ids = step_ids(0, LENGTH, 2 * COL).astype(f32)
    growth = jnp.exp(ids * -LOG_STEP)
    seconds = []
    for dz in range(2):
        residues = []
        for dy in range(2):
            pair = 2 * dz + dy
            around = jnp.concatenate(
                [
                    lows[pair],
                    lows[2 - 2 * dz + dy],
                    lows[2 * dz + 1 - dy],
                    lows[4 + 2 * dz + dy],
                    lows[8 + dz],
                    lows[10 + dz],
                ],
                axis=1,
            )
            image = dot(around, ops[pair])
            earlier = pltpu.roll(image[:, COL:], 1, 0)
            residue = fields(pair, 1).astype(f32) - image[:, :COL] + MODULUS * earlier
            residues.append(residue.astype(bf16))
        second = firsts[dz] + dot(jnp.concatenate(residues, axis=1), diagonals[dz])
        in_time = (second * growth).astype(bf16)
        for dest in range(PARTS):
            out[dest, 2 * STEPS :, 2 * dz * COL : 2 * (dz + 1) * COL] = in_time[
                dest * STEPS : (dest + 1) * STEPS
            ]
        seconds.append(second)
    second = jnp.concatenate(seconds, axis=1)
    high = second.astype(bf16)
    rest = (second - high.astype(f32)).astype(bf16)
    spectrum = dot(table[...], jnp.concatenate([high, rest, high], axis=0)).astype(bf16)
    for dest in range(PARTS):
        out[dest, : 2 * STEPS] = spectrum[dest * 2 * STEPS : (dest + 1) * 2 * STEPS]


def solve(recv, ops, box):
    return pl.pallas_call(
        solve_kernel,
        out_shape=jax.ShapeDtypeStruct((PARTS, 3 * STEPS, OWN), bf16),
        name="solve",
        compiler_params=pltpu.CompilerParams(vmem_limit_bytes=16 * 2**20),
        cost_estimate=cost(3 * 10**9, 5 * 10**6),
    )(recv, ops, box, jnp.asarray(dft_table()))


def unpack_kernel(recv, real, imag, in_time, ready, sems):
    copies = []
    for zg in range(4):
        for which, out in enumerate((real, imag, in_time)):
            for d in range(2):
                for rest in range(4):
                    source = 4 * zg + rest
                    _, yg, xg = box_of(source)
                    for e in range(2):
                        at = (2 * zg + d) * LAYER + (2 * yg + e) * ROW + xg * COL
                        c = 2 * d + e
                        ready[which, :, at : at + COL] = recv[
                            source,
                            which * STEPS : (which + 1) * STEPS,
                            c * COL : (c + 1) * COL,
                        ].astype(f32)
            cut = pl.ds(2 * zg * LAYER, 2 * LAYER)
            copy = pltpu.make_async_copy(
                ready.at[which, :, cut], out.at[:, cut], sems.at[len(copies)]
            )
            copy.start()
            copies.append(copy)
    for copy in copies:
        copy.wait()


def unpack(recv):
    out = jax.ShapeDtypeStruct((STEPS, SLAB), f32)
    return pl.pallas_call(
        unpack_kernel,
        out_shape=(out, out, out),
        out_specs=(pl.BlockSpec(memory_space=pltpu.HBM),) * 3,
        scratch_shapes=[pltpu.VMEM((3, STEPS, SLAB), f32), pltpu.SemaphoreType.DMA((12,))],
        name="unpack",
        compiler_params=pltpu.CompilerParams(vmem_limit_bytes=6 * 2**20),
        cost_estimate=cost(10**6, 3 * 10**6),
    )(recv)


def per_device(forcing, op_main, op_mass, jacobi_inv):
    count = lax.axis_size("space")
    across = [(i, i + 1) for i in range(1, count - 1, 2)]
    within = [(i, i + 1) for i in range(0, count, 2)]
    across += [(j, i) for i, j in across]
    within += [(j, i) for i, j in within]
    jac = jnp.transpose(jacobi_inv, (1, 2, 0))
    forcing = pltpu.with_memory_space_constraint(forcing, pltpu.HBM)
    far, near, held = edges(forcing, pltpu.with_memory_space_constraint(jac, pltpu.HBM))
    far = lax.ppermute(far, "space", across)
    near = lax.ppermute(near, "space", within)
    packed = pack(pltpu.with_memory_space_constraint(held, pltpu.VMEM))
    far, near, packed = lax.optimization_barrier((far, near, packed))
    packed = patch(packed, far, near)
    packed, op_main, op_mass = lax.optimization_barrier((packed, op_main, op_mass))
    recv = lax.all_to_all(packed, "tm", 0, 0).reshape(LENGTH, BOX)
    ops = select_ops(jnp.transpose(op_main, (1, 2, 0)), jnp.transpose(op_mass, (1, 2, 0)))
    ops, jac = lax.optimization_barrier((ops, jac))
    box = select_jac(jac, far, near)
    sent = solve(recv, ops, box)
    back = lax.all_to_all(sent, "tm", 0, 0)
    return unpack(back)


def solution(mesh):
    in_specs = (
        P("tm", "space"),
        P("space", None, None),
        P("space", None, None),
        P("space", None, None),
    )
    out_specs = (P("tm", "space"), P("tm", "space"), P("tm", "space"))
    return jax.shard_map(
        per_device, mesh=mesh, in_specs=in_specs, out_specs=out_specs, check_vma=False
    )
```

```python
import functools
import math

import jax
import jax.numpy as jnp
import ml_dtypes
import numpy as np
from jax import lax
from jax.experimental import pallas as pl
from jax.experimental.pallas import tpu as pltpu
from jax.sharding import PartitionSpec as P

LENGTH = 256
PARTS = 16
STEPS = LENGTH // PARTS
BS = 64
LAYER = 1024
ROW = 256
LAYERS = 8
SLAB = LAYERS * LAYER
BLOCKS = SLAB // BS
SLOTS = 7
COL = 128
OWN = 4 * COL
BOX = 12 * COL
CHUNK = 16

ALPHA = 0.25
LOG_STEP = math.log(ALPHA) / LENGTH
MODULUS = ALPHA ** (1.0 / LENGTH)

f32 = jnp.float32
bf16 = jnp.bfloat16


def box_of(part):
    return part // 4, part // 2 % 2, part % 2


def dft_table():
    freq = np.arange(LENGTH)[:, None]
    step = np.arange(LENGTH)[None, :]
    angle = 2.0 * np.pi * (freq * step % LENGTH) / LENGTH
    table = np.stack([np.cos(angle), -np.sin(angle)], 1) / math.sqrt(LENGTH)
    table = table.reshape(PARTS, STEPS, 2, LENGTH).transpose(0, 2, 1, 3)
    table = table.reshape(2 * LENGTH, LENGTH)
    high = table.astype(ml_dtypes.bfloat16)
    low = (table - high.astype(np.float64)).astype(ml_dtypes.bfloat16)
    return np.concatenate([high, high, low], axis=1)


def step_ids(part, count, width):
    return part * STEPS + lax.broadcasted_iota(jnp.int32, (count, width), 0)


def cost(flops, nbytes):
    return pl.CostEstimate(flops=flops, bytes_accessed=nbytes, transcendentals=0)


def dot(a, b):
    return jnp.dot(a, b, preferred_element_type=f32)


def scales():
    ids = step_ids(lax.axis_index("tm"), STEPS, COL).astype(f32)
    return jnp.exp(ids * LOG_STEP)


def pack_kernel(forcing, out):
    scale = scales()
    half = lax.broadcasted_iota(jnp.int32, (STEPS, COL), 1) < BS

    def column(z, y, x):
        at = z * LAYER + y * ROW + x * COL
        return forcing[:, at : at + COL] * scale

    def put(dest, c, value):
        out[dest, :, c * COL : (c + 1) * COL] = value.astype(bf16)

    for dest in range(PARTS):
        zg, yg, xg = box_of(dest)
        for d in range(2):
            for e in range(2):
                put(dest, 2 * d + e, column(2 * zg + d, 2 * yg + e, xg))
            y = 2 * yg + d
            if zg > 0:
                put(dest, 4 + d, column(2 * zg - 1, y, xg))
            if zg < 3:
                put(dest, 6 + d, column(2 * zg + 2, y, xg))
            z = 2 * zg + d
            put(dest, 8 + d, column(z, 2 - yg, xg))
            first = column(z, 2 * yg, 1 - xg)
            second = column(z, 2 * yg + 1, 1 - xg)
            if xg == 0:
                pair = jnp.where(half, first, pltpu.roll(second, BS, 1))
            else:
                pair = jnp.where(half, pltpu.roll(first, BS, 1), second)
            put(dest, 10 + d, pair)


def pack(forcing):
    return pl.pallas_call(
        pack_kernel,
        in_specs=[pl.BlockSpec(memory_space=pltpu.VMEM)],
        out_shape=jax.ShapeDtypeStruct((PARTS, STEPS, BOX), bf16),
        name="pack",
        compiler_params=pltpu.CompilerParams(vmem_limit_bytes=6 * 2**20),
        cost_estimate=cost(10**6, 4 * 10**6),
    )(forcing)


def patch_kernel(packed, far, near, out, sems):
    def place(low_edge, high_edge):
        copies = [
            pltpu.make_async_copy(
                edge.at[pl.ds(0, 4)],
                out.at[pl.ds(first_dest, 4), :, pl.ds(first * COL, 2 * COL)],
                sems.at[which],
            )
            for which, (edge, first_dest, first) in enumerate(
                ((low_edge, 0, 4), (high_edge, PARTS - 4, 6))
            )
        ]
        for copy in copies:
            copy.start()
        for copy in copies:
            copy.wait()

    core = lax.axis_index("space") % 2

    @pl.when(core == 0)
    def _():
        place(far, near)

    @pl.when(core == 1)
    def _():
        place(near, far)


def patch(packed, far, near):
    anywhere = pl.BlockSpec(memory_space=pl.ANY)
    return pl.pallas_call(
        patch_kernel,
        in_specs=[anywhere] * 3,
        out_specs=anywhere,
        out_shape=jax.ShapeDtypeStruct((PARTS, STEPS, BOX), bf16),
        scratch_shapes=[pltpu.SemaphoreType.DMA((2,))],
        input_output_aliases={0: 0},
        name="patch",
        compiler_params=pltpu.CompilerParams(vmem_limit_bytes=2**20),
        cost_estimate=cost(10**3, 2 * 10**5),
    )(packed, far, near)


def selector(blocks, width):
    block = lax.broadcasted_iota(jnp.int32, (BLOCKS, width), 0)
    lane = lax.broadcasted_iota(jnp.int32, (BLOCKS, width), 1)
    hit = block == blocks
    pieces = [
        jnp.where(hit & (lane % CHUNK == o), 1.0, 0.0).astype(bf16) for o in range(CHUNK)
    ]
    return jnp.concatenate(pieces, axis=0)


def reorder(width):
    slots = width // BS
    source = lax.broadcasted_iota(jnp.int32, (width, width), 0)
    lane = lax.broadcasted_iota(jnp.int32, (width, width), 1)
    wanted = lane % BS // CHUNK * (slots * CHUNK) + lane // BS * CHUNK + lane % CHUNK
    return jnp.where(source == wanted, 1.0, 0.0).astype(bf16)


def select_chunk(read, chosen):
    rows = jnp.concatenate([read(o) for o in range(CHUNK)], axis=1)
    return dot(rows, chosen).astype(bf16)


def select_all(jac, chosen, perm):
    chunks = BS // CHUNK
    rows = jnp.concatenate(
        [
            jnp.concatenate([jac[c * CHUNK + o] for c in range(chunks)], axis=0)
            for o in range(CHUNK)
        ],
        axis=1,
    )
    picked = dot(rows, chosen).astype(bf16)
    side = jnp.concatenate([picked[c * BS : (c + 1) * BS] for c in range(chunks)], axis=1)
    return dot(side, perm).astype(bf16)


def slots_of():
    return lax.broadcasted_iota(jnp.int32, (1, COL), 1) // CHUNK


def block_at(z, y, x):
    return z * 16 + y * 4 + x


def edge_kernel(forcing, jac, far, near, held, local, sems):
    _, yg, xg = box_of(lax.axis_index("tm"))
    near_layer = jnp.where(lax.axis_index("space") % 2 == 0, LAYERS - 1, 0)
    first, middle, last = LAYER, SLAB - 2 * LAYER, LAYER
    cuts = [pl.ds(0, first), pl.ds(SLAB - last, last), pl.ds(first, middle)]
    copies = [
        pltpu.make_async_copy(forcing.at[:, cut], held.at[:, cut], sems.at[which])
        for which, cut in enumerate(cuts)
    ]
    for c in range(BS // CHUNK):
        cut = pl.ds(c * CHUNK, CHUNK)
        copies.append(pltpu.make_async_copy(jac.at[cut], local.at[cut], sems.at[3 + c]))
    for which in (0, 1, 3, 4, 5, 6, 2):
        copies[which].start()
    scale = scales()
    slot = slots_of()
    layer = jnp.where(slot < 4, near_layer, LAYERS - 1 - near_layer)
    chosen = selector(
        block_at(layer, 2 * yg + slot // 2 % 2, 2 * xg + slot % 2), COL
    )
    perm = reorder(4 * COL)
    copies[0].wait()
    copies[1].wait()
    even = near_layer > 0
    for target in range(4):
        for d in range(2):
            at = (2 * (target // 2) + d) * ROW + target % 2 * COL
            to = slice(d * COL, (d + 1) * COL)
            bottom = (held[:, at : at + COL] * scale).astype(bf16)
            at += SLAB - LAYER
            top = (held[:, at : at + COL] * scale).astype(bf16)
            near[target, :, to] = jnp.where(even, top, bottom)
            far[target, :, to] = jnp.where(even, bottom, top)
    for c in range(BS // CHUNK):
        copies[3 + c].wait()
    picked = select_all(local, chosen, perm)
    for a in range(BS // STEPS):
        rows = slice(a * STEPS, (a + 1) * STEPS)
        near[4 + a] = picked[rows, : 2 * COL]
        far[4 + a] = picked[rows, 2 * COL :]
    copies[2].wait()


def edges(forcing, jac):
    edge = jax.ShapeDtypeStruct((4 + BS // STEPS, STEPS, 2 * COL), bf16)
    hbm = pl.BlockSpec(memory_space=pltpu.HBM)
    return pl.pallas_call(
        edge_kernel,
        in_specs=[hbm, hbm],
        out_shape=(edge, edge, jax.ShapeDtypeStruct((STEPS, SLAB), f32)),
        scratch_shapes=[
            pltpu.VMEM((BS, BS, BLOCKS), bf16),
            pltpu.SemaphoreType.DMA((7,)),
        ],
        name="edges",
        compiler_params=pltpu.CompilerParams(vmem_limit_bytes=6 * 2**20),
        cost_estimate=cost(10**8, 2 * 10**6),
    )(forcing, jac)


def jac_kernel(jac, far, near, box, local, sem):
    copy = pltpu.make_async_copy(jac, local, sem)
    copy.start()
    zg, yg, xg = box_of(lax.axis_index("tm"))
    slot = slots_of()
    d = slot // 2 % 2
    e = slot % 2
    first = slot < 4
    own = block_at(2 * zg + slot // 4, 2 * yg + d, 2 * xg + e)
    layer = jnp.where(
        first, jnp.maximum(2 * zg - 1, 0), jnp.minimum(2 * zg + 2, LAYERS - 1)
    )
    faces = block_at(layer, 2 * yg + d, 2 * xg + e)
    beside = block_at(2 * zg + d, 2 - yg, 2 * xg + e)
    ahead = block_at(2 * zg + d, 2 * yg + e, 2 - xg)
    perm = reorder(4 * COL)
    copy.wait()
    even = lax.axis_index("space") % 2 == 0

    def other(edge):
        return jnp.concatenate([edge[4 + a] for a in range(BS // STEPS)], axis=0)

    near, far = other(near), other(far)
    for at, blocks in enumerate((own, faces, jnp.where(first, beside, ahead))):
        both = select_all(local, selector(blocks, COL), perm)
        for which in range(2):
            value = both[:, which * 2 * COL : (which + 1) * 2 * COL]
            if at == 1 and which == 0:
                value = jnp.where(zg == 0, jnp.where(even, far, near), value)
            if at == 1 and which == 1:
                value = jnp.where(zg == 3, jnp.where(even, near, far), value)
            p = 2 * at + which
            box[:, 2 * p * COL : 2 * (p + 1) * COL] = value


def select_jac(jac, far, near):
    vmem = pl.BlockSpec(memory_space=pltpu.VMEM)
    return pl.pallas_call(
        jac_kernel,
        in_specs=[pl.BlockSpec(memory_space=pltpu.HBM), vmem, vmem],
        out_shape=jax.ShapeDtypeStruct((BS, BOX), bf16),
        scratch_shapes=[pltpu.VMEM((BS, BS, BLOCKS), bf16), pltpu.SemaphoreType.DMA],
        name="select_jac",
        compiler_params=pltpu.CompilerParams(vmem_limit_bytes=8 * 2**20),
        cost_estimate=cost(10**9, 2 * 10**6),
    )(jac, far, near)


def ops_kernel(main, mass, out, chosen, picked):
    step = pl.program_id(0)
    zg, yg, xg = box_of(lax.axis_index("tm"))

    @pl.when(step == 0)
    def _():
        slot = slots_of()
        blocks = block_at(2 * zg + slot // 4, 2 * yg + slot // 2 % 2, 2 * xg + slot % 2)
        chosen[...] = selector(blocks, COL)

    for which, source in enumerate((main, mass)):
        picked[which, step] = select_chunk(lambda o: source[o], chosen[...])

    @pl.when(step == BS // CHUNK - 1)
    def _():
        perm = reorder(4 * COL)
        both = [
            dot(
                jnp.concatenate([picked[which, c] for c in range(BS // CHUNK)], axis=1), perm
            )
            for which in range(2)
        ]
        lane = lax.broadcasted_iota(jnp.int32, (BS, 2 * COL), 1)
        low = lane % COL < BS
        zero = jnp.zeros((BS, 2 * COL), f32)
        for dz in range(2):
            for dy in range(2):
                pair = 2 * dz + dy
                cut = slice(pair * COL, (pair + 1) * COL)
                slots = [
                    jnp.concatenate([b[s * BS : (s + 1) * BS, cut] for b in both], axis=1)
                    for s in range(SLOTS)
                ]

                def put(at, value):
                    out[pair, at * BS : (at + 1) * BS] = value.astype(bf16)

                def diagonal(at, value):
                    put(at, jnp.where(low, value, zero))
                    put(at + 1, jnp.where(low, zero, value))

                put(0, jnp.where(low, slots[0], slots[1]))
                put(1, jnp.where(low, slots[2], slots[0]))
                diagonal(2, slots[6 - dz])
                diagonal(4, slots[4 - dy])
                diagonal(6, slots[5 + dz])
                faces = (yg == 1) if dy == 0 else (yg == 0)
                diagonal(8, slots[3 + dy] * jnp.where(faces, 1.0, 0.0))
                after = jnp.where(xg == 0, 1.0, 0.0)
                put(
                    10 + dy,
                    jnp.where(low, slots[1] * (1.0 - after), slots[2] * after),
                )
                put(11 - dy, zero)


def select_ops(main, mass):
    spec = pl.BlockSpec((CHUNK, SLOTS * BS, BLOCKS), lambda c: (c, 0, 0))
    return pl.pallas_call(
        ops_kernel,
        grid=(BS // CHUNK,),
        in_specs=[spec, spec],
        out_specs=pl.BlockSpec((4, 6 * COL, 2 * COL), lambda c: (0, 0, 0)),
        out_shape=jax.ShapeDtypeStruct((4, 6 * COL, 2 * COL), bf16),
        scratch_shapes=[
            pltpu.VMEM((CHUNK * BLOCKS, COL), bf16),
            pltpu.VMEM((2, BS // CHUNK, SLOTS * BS, COL), bf16),
        ],
        name="select_ops",
        compiler_params=pltpu.CompilerParams(vmem_limit_bytes=52 * 2**20),
        cost_estimate=cost(4 * 10**9, 16 * 10**6),
    )(main, mass)


def solve_kernel(recv, ops, box, table, out):
    lane = lax.broadcasted_iota(jnp.int32, (BS, 2 * COL), 1) // BS

    def diagonal(p):
        value = box[:, 2 * p * COL : 2 * (p + 1) * COL]
        rows = [jnp.where(lane == q, value, jnp.zeros_like(value)) for q in range(4)]
        return jnp.concatenate(rows, axis=0)

    diagonals = [diagonal(p) for p in range(6)]

    def fields(c, count):
        return recv[:, c * COL : (c + count) * COL]

    firsts = [dot(fields(2 * p, 2), diagonals[p]) for p in range(2)]
    halves = [value.astype(bf16) for value in firsts]
    halves += [dot(fields(2 * p, 2), diagonals[p]).astype(bf16) for p in range(2, 6)]
    lows = [half[:, e * COL : (e + 1) * COL] for half in halves for e in range(2)]

    ids = step_ids(0, LENGTH, 2 * COL).astype(f32)
    growth = jnp.exp(ids * -LOG_STEP)
    seconds = []
    for dz in range(2):
        residues = []
        for dy in range(2):
            pair = 2 * dz + dy
            around = jnp.concatenate(
                [
                    lows[pair],
                    lows[2 - 2 * dz + dy],
                    lows[2 * dz + 1 - dy],
                    lows[4 + 2 * dz + dy],
                    lows[8 + dz],
                    lows[10 + dz],
                ],
                axis=1,
            )
            image = dot(around, ops[pair])
            earlier = pltpu.roll(image[:, COL:], 1, 0)
            residue = fields(pair, 1).astype(f32) - image[:, :COL] + MODULUS * earlier
            residues.append(residue.astype(bf16))
        second = firsts[dz] + dot(jnp.concatenate(residues, axis=1), diagonals[dz])
        in_time = (second * growth).astype(bf16)
        for dest in range(PARTS):
            out[dest, 2 * STEPS :, 2 * dz * COL : 2 * (dz + 1) * COL] = in_time[
                dest * STEPS : (dest + 1) * STEPS
            ]
        seconds.append(second)
    second = jnp.concatenate(seconds, axis=1)
    high = second.astype(bf16)
    rest = (second - high.astype(f32)).astype(bf16)
    spectrum = dot(table[...], jnp.concatenate([high, rest, high], axis=0)).astype(bf16)
    for dest in range(PARTS):
        out[dest, : 2 * STEPS] = spectrum[dest * 2 * STEPS : (dest + 1) * 2 * STEPS]


def solve(recv, ops, box):
    return pl.pallas_call(
        solve_kernel,
        out_shape=jax.ShapeDtypeStruct((PARTS, 3 * STEPS, OWN), bf16),
        name="solve",
        compiler_params=pltpu.CompilerParams(vmem_limit_bytes=16 * 2**20),
        cost_estimate=cost(3 * 10**9, 5 * 10**6),
    )(recv, ops, box, jnp.asarray(dft_table()))


def unpack_kernel(recv, real, imag, in_time, ready, sems):
    copies = []
    for zg in range(4):
        for which, out in enumerate((real, imag, in_time)):
            for d in range(2):
                for rest in range(4):
                    source = 4 * zg + rest
                    _, yg, xg = box_of(source)
                    for e in range(2):
                        at = (2 * zg + d) * LAYER + (2 * yg + e) * ROW + xg * COL
                        c = 2 * d + e
                        ready[which, :, at : at + COL] = recv[
                            source,
                            which * STEPS : (which + 1) * STEPS,
                            c * COL : (c + 1) * COL,
                        ].astype(f32)
            cut = pl.ds(2 * zg * LAYER, 2 * LAYER)
            copy = pltpu.make_async_copy(
                ready.at[which, :, cut], out.at[:, cut], sems.at[len(copies)]
            )
            copy.start()
            copies.append(copy)
    for copy in copies:
        copy.wait()


def unpack(recv):
    out = jax.ShapeDtypeStruct((STEPS, SLAB), f32)
    return pl.pallas_call(
        unpack_kernel,
        out_shape=(out, out, out),
        out_specs=(pl.BlockSpec(memory_space=pltpu.HBM),) * 3,
        scratch_shapes=[pltpu.VMEM((3, STEPS, SLAB), f32), pltpu.SemaphoreType.DMA((12,))],
        name="unpack",
        compiler_params=pltpu.CompilerParams(vmem_limit_bytes=6 * 2**20),
        cost_estimate=cost(10**6, 3 * 10**6),
    )(recv)


def per_device(forcing, op_main, op_mass, jacobi_inv):
    count = lax.axis_size("space")
    across = [(i, i + 1) for i in range(1, count - 1, 2)]
    within = [(i, i + 1) for i in range(0, count, 2)]
    across += [(j, i) for i, j in across]
    within += [(j, i) for i, j in within]
    jac = jnp.transpose(jacobi_inv, (1, 2, 0))
    forcing = pltpu.with_memory_space_constraint(forcing, pltpu.HBM)
    far, near, held = edges(forcing, pltpu.with_memory_space_constraint(jac, pltpu.HBM))
    far = lax.ppermute(far, "space", across)
    near = lax.ppermute(near, "space", within)
    packed = pack(pltpu.with_memory_space_constraint(held, pltpu.VMEM))
    far, near, packed = lax.optimization_barrier((far, near, packed))
    packed = patch(packed, far, near)
    packed, op_main, op_mass = lax.optimization_barrier((packed, op_main, op_mass))
    recv = lax.all_to_all(packed, "tm", 0, 0).reshape(LENGTH, BOX)
    ops = select_ops(jnp.transpose(op_main, (1, 2, 0)), jnp.transpose(op_mass, (1, 2, 0)))
    ops, jac = lax.optimization_barrier((ops, jac))
    box = select_jac(jac, far, near)
    sent = solve(recv, ops, box)
    back = lax.all_to_all(sent, "tm", 0, 0)
    return unpack(back)


def solution(mesh):
    in_specs = (
        P("tm", "space"),
        P("space", None, None),
        P("space", None, None),
        P("space", None, None),
    )
    out_specs = (P("tm", "space"), P("tm", "space"), P("tm", "space"))
    return jax.shard_map(
        per_device, mesh=mesh, in_specs=in_specs, out_specs=out_specs, check_vma=False
    )
```

```python
import functools
import math

import jax
import jax.numpy as jnp
import ml_dtypes
import numpy as np
from jax import lax
from jax.experimental import pallas as pl
from jax.experimental.pallas import tpu as pltpu
from jax.sharding import PartitionSpec as P

LENGTH = 256
PARTS = 16
STEPS = LENGTH // PARTS
BS = 64
LAYER = 1024
ROW = 256
LAYERS = 8
SLAB = LAYERS * LAYER
BLOCKS = SLAB // BS
SLOTS = 7
COL = 128
OWN = 4 * COL
BOX = 12 * COL
CHUNK = 16

ALPHA = 0.25
LOG_STEP = math.log(ALPHA) / LENGTH
MODULUS = ALPHA ** (1.0 / LENGTH)

f32 = jnp.float32
bf16 = jnp.bfloat16


def box_of(part):
    return part // 4, part // 2 % 2, part % 2


def dft_table():
    freq = np.arange(LENGTH)[:, None]
    step = np.arange(LENGTH)[None, :]
    angle = 2.0 * np.pi * (freq * step % LENGTH) / LENGTH
    table = np.stack([np.cos(angle), -np.sin(angle)], 1) / math.sqrt(LENGTH)
    table = table.reshape(PARTS, STEPS, 2, LENGTH).transpose(0, 2, 1, 3)
    table = table.reshape(2 * LENGTH, LENGTH)
    high = table.astype(ml_dtypes.bfloat16)
    low = (table - high.astype(np.float64)).astype(ml_dtypes.bfloat16)
    return np.concatenate([high, high, low], axis=1)


def step_ids(part, count, width):
    return part * STEPS + lax.broadcasted_iota(jnp.int32, (count, width), 0)


def cost(flops, nbytes):
    return pl.CostEstimate(flops=flops, bytes_accessed=nbytes, transcendentals=0)


def dot(a, b):
    return jnp.dot(a, b, preferred_element_type=f32)


def scales():
    ids = step_ids(lax.axis_index("tm"), STEPS, COL).astype(f32)
    return jnp.exp(ids * LOG_STEP)


def pack_kernel(forcing, out):
    scale = scales()
    half = lax.broadcasted_iota(jnp.int32, (STEPS, COL), 1) < BS

    def column(z, y, x):
        at = z * LAYER + y * ROW + x * COL
        return forcing[:, at : at + COL] * scale

    def put(dest, c, value):
        out[dest, :, c * COL : (c + 1) * COL] = value.astype(bf16)

    for dest in range(PARTS):
        zg, yg, xg = box_of(dest)
        for d in range(2):
            for e in range(2):
                put(dest, 2 * d + e, column(2 * zg + d, 2 * yg + e, xg))
            y = 2 * yg + d
            if zg > 0:
                put(dest, 4 + d, column(2 * zg - 1, y, xg))
            if zg < 3:
                put(dest, 6 + d, column(2 * zg + 2, y, xg))
            z = 2 * zg + d
            put(dest, 8 + d, column(z, 2 - yg, xg))
            first = column(z, 2 * yg, 1 - xg)
            second = column(z, 2 * yg + 1, 1 - xg)
            if xg == 0:
                pair = jnp.where(half, first, pltpu.roll(second, BS, 1))
            else:
                pair = jnp.where(half, pltpu.roll(first, BS, 1), second)
            put(dest, 10 + d, pair)


def pack(forcing):
    return pl.pallas_call(
        pack_kernel,
        in_specs=[pl.BlockSpec(memory_space=pltpu.VMEM)],
        out_shape=jax.ShapeDtypeStruct((PARTS, STEPS, BOX), bf16),
        name="pack",
        compiler_params=pltpu.CompilerParams(vmem_limit_bytes=6 * 2**20),
        cost_estimate=cost(10**6, 4 * 10**6),
    )(forcing)


def patch_kernel(packed, far, near, out, sems):
    def place(low_edge, high_edge):
        copies = [
            pltpu.make_async_copy(
                edge.at[pl.ds(0, 4)],
                out.at[pl.ds(first_dest, 4), :, pl.ds(first * COL, 2 * COL)],
                sems.at[which],
            )
            for which, (edge, first_dest, first) in enumerate(
                ((low_edge, 0, 4), (high_edge, PARTS - 4, 6))
            )
        ]
        for copy in copies:
            copy.start()
        for copy in copies:
            copy.wait()

    core = lax.axis_index("space") % 2

    @pl.when(core == 0)
    def _():
        place(far, near)

    @pl.when(core == 1)
    def _():
        place(near, far)


def patch(packed, far, near):
    anywhere = pl.BlockSpec(memory_space=pl.ANY)
    return pl.pallas_call(
        patch_kernel,
        in_specs=[anywhere] * 3,
        out_specs=anywhere,
        out_shape=jax.ShapeDtypeStruct((PARTS, STEPS, BOX), bf16),
        scratch_shapes=[pltpu.SemaphoreType.DMA((2,))],
        input_output_aliases={0: 0},
        name="patch",
        compiler_params=pltpu.CompilerParams(vmem_limit_bytes=2**20),
        cost_estimate=cost(10**3, 2 * 10**5),
    )(packed, far, near)


def selector(blocks, width):
    block = lax.broadcasted_iota(jnp.int32, (BLOCKS, width), 0)
    lane = lax.broadcasted_iota(jnp.int32, (BLOCKS, width), 1)
    hit = block == blocks
    pieces = [
        jnp.where(hit & (lane % CHUNK == o), 1.0, 0.0).astype(bf16) for o in range(CHUNK)
    ]
    return jnp.concatenate(pieces, axis=0)


def reorder(width):
    slots = width // BS
    source = lax.broadcasted_iota(jnp.int32, (width, width), 0)
    lane = lax.broadcasted_iota(jnp.int32, (width, width), 1)
    wanted = lane % BS // CHUNK * (slots * CHUNK) + lane // BS * CHUNK + lane % CHUNK
    return jnp.where(source == wanted, 1.0, 0.0).astype(bf16)


def select_chunk(read, chosen):
    rows = jnp.concatenate([read(o) for o in range(CHUNK)], axis=1)
    return dot(rows, chosen).astype(bf16)


def select_all(jac, chosen, perm):
    chunks = BS // CHUNK
    rows = jnp.concatenate(
        [
            jnp.concatenate([jac[c * CHUNK + o] for c in range(chunks)], axis=0)
            for o in range(CHUNK)
        ],
        axis=1,
    )
    picked = dot(rows, chosen).astype(bf16)
    side = jnp.concatenate([picked[c * BS : (c + 1) * BS] for c in range(chunks)], axis=1)
    return dot(side, perm).astype(bf16)


def slots_of():
    return lax.broadcasted_iota(jnp.int32, (1, COL), 1) // CHUNK


def block_at(z, y, x):
    return z * 16 + y * 4 + x


def edge_kernel(forcing, jac, far, near, held, local, sems):
    _, yg, xg = box_of(lax.axis_index("tm"))
    near_layer = jnp.where(lax.axis_index("space") % 2 == 0, LAYERS - 1, 0)
    first, middle, last = LAYER, SLAB - 2 * LAYER, LAYER
    cuts = [pl.ds(0, first), pl.ds(SLAB - last, last), pl.ds(first, middle)]
    copies = [
        pltpu.make_async_copy(forcing.at[:, cut], held.at[:, cut], sems.at[which])
        for which, cut in enumerate(cuts)
    ]
    for c in range(BS // CHUNK):
        cut = pl.ds(c * CHUNK, CHUNK)
        copies.append(pltpu.make_async_copy(jac.at[cut], local.at[cut], sems.at[3 + c]))
    for which in (3, 4, 5, 6, 0, 1, 2):
        copies[which].start()
    scale = scales()
    slot = slots_of()
    layer = jnp.where(slot < 4, near_layer, LAYERS - 1 - near_layer)
    chosen = selector(
        block_at(layer, 2 * yg + slot // 2 % 2, 2 * xg + slot % 2), COL
    )
    perm = reorder(4 * COL)
    copies[0].wait()
    copies[1].wait()
    even = near_layer > 0
    for target in range(4):
        for d in range(2):
            at = (2 * (target // 2) + d) * ROW + target % 2 * COL
            to = slice(d * COL, (d + 1) * COL)
            bottom = (held[:, at : at + COL] * scale).astype(bf16)
            at += SLAB - LAYER
            top = (held[:, at : at + COL] * scale).astype(bf16)
            near[target, :, to] = jnp.where(even, top, bottom)
            far[target, :, to] = jnp.where(even, bottom, top)
    for c in range(BS // CHUNK):
        copies[3 + c].wait()
    picked = select_all(local, chosen, perm)
    for a in range(BS // STEPS):
        rows = slice(a * STEPS, (a + 1) * STEPS)
        near[4 + a] = picked[rows, : 2 * COL]
        far[4 + a] = picked[rows, 2 * COL :]
    copies[2].wait()


def edges(forcing, jac):
    edge = jax.ShapeDtypeStruct((4 + BS // STEPS, STEPS, 2 * COL), bf16)
    hbm = pl.BlockSpec(memory_space=pltpu.HBM)
    return pl.pallas_call(
        edge_kernel,
        in_specs=[hbm, hbm],
        out_shape=(edge, edge, jax.ShapeDtypeStruct((STEPS, SLAB), f32)),
        scratch_shapes=[
            pltpu.VMEM((BS, BS, BLOCKS), bf16),
            pltpu.SemaphoreType.DMA((7,)),
        ],
        name="edges",
        compiler_params=pltpu.CompilerParams(vmem_limit_bytes=6 * 2**20),
        cost_estimate=cost(10**8, 2 * 10**6),
    )(forcing, jac)


def jac_kernel(jac, far, near, box, local, sem):
    copy = pltpu.make_async_copy(jac, local, sem)
    copy.start()
    zg, yg, xg = box_of(lax.axis_index("tm"))
    slot = slots_of()
    d = slot // 2 % 2
    e = slot % 2
    first = slot < 4
    own = block_at(2 * zg + slot // 4, 2 * yg + d, 2 * xg + e)
    layer = jnp.where(
        first, jnp.maximum(2 * zg - 1, 0), jnp.minimum(2 * zg + 2, LAYERS - 1)
    )
    faces = block_at(layer, 2 * yg + d, 2 * xg + e)
    beside = block_at(2 * zg + d, 2 - yg, 2 * xg + e)
    ahead = block_at(2 * zg + d, 2 * yg + e, 2 - xg)
    perm = reorder(4 * COL)
    copy.wait()
    even = lax.axis_index("space") % 2 == 0

    def other(edge):
        return jnp.concatenate([edge[4 + a] for a in range(BS // STEPS)], axis=0)

    near, far = other(near), other(far)
    for at, blocks in enumerate((own, faces, jnp.where(first, beside, ahead))):
        both = select_all(local, selector(blocks, COL), perm)
        for which in range(2):
            value = both[:, which * 2 * COL : (which + 1) * 2 * COL]
            if at == 1 and which == 0:
                value = jnp.where(zg == 0, jnp.where(even, far, near), value)
            if at == 1 and which == 1:
                value = jnp.where(zg == 3, jnp.where(even, near, far), value)
            p = 2 * at + which
            box[:, 2 * p * COL : 2 * (p + 1) * COL] = value


def select_jac(jac, far, near):
    vmem = pl.BlockSpec(memory_space=pltpu.VMEM)
    return pl.pallas_call(
        jac_kernel,
        in_specs=[pl.BlockSpec(memory_space=pltpu.HBM), vmem, vmem],
        out_shape=jax.ShapeDtypeStruct((BS, BOX), bf16),
        scratch_shapes=[pltpu.VMEM((BS, BS, BLOCKS), bf16), pltpu.SemaphoreType.DMA],
        name="select_jac",
        compiler_params=pltpu.CompilerParams(vmem_limit_bytes=8 * 2**20),
        cost_estimate=cost(10**9, 2 * 10**6),
    )(jac, far, near)


def ops_kernel(main, mass, out, chosen, picked):
    step = pl.program_id(0)
    zg, yg, xg = box_of(lax.axis_index("tm"))

    @pl.when(step == 0)
    def _():
        slot = slots_of()
        blocks = block_at(2 * zg + slot // 4, 2 * yg + slot // 2 % 2, 2 * xg + slot % 2)
        chosen[...] = selector(blocks, COL)

    for which, source in enumerate((main, mass)):
        picked[which, step] = select_chunk(lambda o: source[o], chosen[...])

    @pl.when(step == BS // CHUNK - 1)
    def _():
        perm = reorder(4 * COL)
        both = [
            dot(
                jnp.concatenate([picked[which, c] for c in range(BS // CHUNK)], axis=1), perm
            )
            for which in range(2)
        ]
        lane = lax.broadcasted_iota(jnp.int32, (BS, 2 * COL), 1)
        low = lane % COL < BS
        zero = jnp.zeros((BS, 2 * COL), f32)
        for dz in range(2):
            for dy in range(2):
                pair = 2 * dz + dy
                cut = slice(pair * COL, (pair + 1) * COL)
                slots = [
                    jnp.concatenate([b[s * BS : (s + 1) * BS, cut] for b in both], axis=1)
                    for s in range(SLOTS)
                ]

                def put(at, value):
                    out[pair, at * BS : (at + 1) * BS] = value.astype(bf16)

                def diagonal(at, value):
                    put(at, jnp.where(low, value, zero))
                    put(at + 1, jnp.where(low, zero, value))

                put(0, jnp.where(low, slots[0], slots[1]))
                put(1, jnp.where(low, slots[2], slots[0]))
                diagonal(2, slots[6 - dz])
                diagonal(4, slots[4 - dy])
                diagonal(6, slots[5 + dz])
                faces = (yg == 1) if dy == 0 else (yg == 0)
                diagonal(8, slots[3 + dy] * jnp.where(faces, 1.0, 0.0))
                after = jnp.where(xg == 0, 1.0, 0.0)
                put(
                    10 + dy,
                    jnp.where(low, slots[1] * (1.0 - after), slots[2] * after),
                )
                put(11 - dy, zero)


def select_ops(main, mass):
    spec = pl.BlockSpec((CHUNK, SLOTS * BS, BLOCKS), lambda c: (c, 0, 0))
    return pl.pallas_call(
        ops_kernel,
        grid=(BS // CHUNK,),
        in_specs=[spec, spec],
        out_specs=pl.BlockSpec((4, 6 * COL, 2 * COL), lambda c: (0, 0, 0)),
        out_shape=jax.ShapeDtypeStruct((4, 6 * COL, 2 * COL), bf16),
        scratch_shapes=[
            pltpu.VMEM((CHUNK * BLOCKS, COL), bf16),
            pltpu.VMEM((2, BS // CHUNK, SLOTS * BS, COL), bf16),
        ],
        name="select_ops",
        compiler_params=pltpu.CompilerParams(vmem_limit_bytes=52 * 2**20),
        cost_estimate=cost(4 * 10**9, 16 * 10**6),
    )(main, mass)


def solve_kernel(recv, ops, box, table, out):
    lane = lax.broadcasted_iota(jnp.int32, (BS, 2 * COL), 1) // BS

    def diagonal(p):
        value = box[:, 2 * p * COL : 2 * (p + 1) * COL]
        rows = [jnp.where(lane == q, value, jnp.zeros_like(value)) for q in range(4)]
        return jnp.concatenate(rows, axis=0)

    diagonals = [diagonal(p) for p in range(6)]

    def fields(c, count):
        return recv[:, c * COL : (c + count) * COL]

    firsts = [dot(fields(2 * p, 2), diagonals[p]) for p in range(2)]
    halves = [value.astype(bf16) for value in firsts]
    halves += [dot(fields(2 * p, 2), diagonals[p]).astype(bf16) for p in range(2, 6)]
    lows = [half[:, e * COL : (e + 1) * COL] for half in halves for e in range(2)]

    ids = step_ids(0, LENGTH, 2 * COL).astype(f32)
    growth = jnp.exp(ids * -LOG_STEP)
    seconds = []
    for dz in range(2):
        residues = []
        for dy in range(2):
            pair = 2 * dz + dy
            around = jnp.concatenate(
                [
                    lows[pair],
                    lows[2 - 2 * dz + dy],
                    lows[2 * dz + 1 - dy],
                    lows[4 + 2 * dz + dy],
                    lows[8 + dz],
                    lows[10 + dz],
                ],
                axis=1,
            )
            image = dot(around, ops[pair])
            earlier = pltpu.roll(image[:, COL:], 1, 0)
            residue = fields(pair, 1).astype(f32) - image[:, :COL] + MODULUS * earlier
            residues.append(residue.astype(bf16))
        second = firsts[dz] + dot(jnp.concatenate(residues, axis=1), diagonals[dz])
        in_time = (second * growth).astype(bf16)
        for dest in range(PARTS):
            out[dest, 2 * STEPS :, 2 * dz * COL : 2 * (dz + 1) * COL] = in_time[
                dest * STEPS : (dest + 1) * STEPS
            ]
        seconds.append(second)
    second = jnp.concatenate(seconds, axis=1)
    high = second.astype(bf16)
    rest = (second - high.astype(f32)).astype(bf16)
    spectrum = dot(table[...], jnp.concatenate([high, rest, high], axis=0)).astype(bf16)
    for dest in range(PARTS):
        out[dest, : 2 * STEPS] = spectrum[dest * 2 * STEPS : (dest + 1) * 2 * STEPS]


def solve(recv, ops, box):
    return pl.pallas_call(
        solve_kernel,
        out_shape=jax.ShapeDtypeStruct((PARTS, 3 * STEPS, OWN), bf16),
        name="solve",
        compiler_params=pltpu.CompilerParams(vmem_limit_bytes=16 * 2**20),
        cost_estimate=cost(3 * 10**9, 5 * 10**6),
    )(recv, ops, box, jnp.asarray(dft_table()))


def unpack_kernel(recv, real, imag, in_time, ready, sems):
    copies = []
    for z in range(LAYERS):
        zg, d = z // 2, z % 2
        for which, out in enumerate((real, imag, in_time)):
            for rest in range(4):
                source = 4 * zg + rest
                _, yg, xg = box_of(source)
                for e in range(2):
                    at = z * LAYER + (2 * yg + e) * ROW + xg * COL
                    c = 2 * d + e
                    ready[which, :, at : at + COL] = recv[
                        source,
                        which * STEPS : (which + 1) * STEPS,
                        c * COL : (c + 1) * COL,
                    ].astype(f32)
            cut = pl.ds(z * LAYER, LAYER)
            copy = pltpu.make_async_copy(
                ready.at[which, :, cut], out.at[:, cut], sems.at[len(copies)]
            )
            copy.start()
            copies.append(copy)
    for copy in copies:
        copy.wait()


def unpack(recv):
    out = jax.ShapeDtypeStruct((STEPS, SLAB), f32)
    return pl.pallas_call(
        unpack_kernel,
        out_shape=(out, out, out),
        out_specs=(pl.BlockSpec(memory_space=pltpu.HBM),) * 3,
        scratch_shapes=[pltpu.VMEM((3, STEPS, SLAB), f32), pltpu.SemaphoreType.DMA((24,))],
        name="unpack",
        compiler_params=pltpu.CompilerParams(vmem_limit_bytes=6 * 2**20),
        cost_estimate=cost(10**6, 3 * 10**6),
    )(recv)


def per_device(forcing, op_main, op_mass, jacobi_inv):
    count = lax.axis_size("space")
    across = [(i, i + 1) for i in range(1, count - 1, 2)]
    within = [(i, i + 1) for i in range(0, count, 2)]
    across += [(j, i) for i, j in across]
    within += [(j, i) for i, j in within]
    jac = jnp.transpose(jacobi_inv, (1, 2, 0))
    forcing = pltpu.with_memory_space_constraint(forcing, pltpu.HBM)
    far, near, held = edges(forcing, pltpu.with_memory_space_constraint(jac, pltpu.HBM))
    far = lax.ppermute(far, "space", across)
    near = lax.ppermute(near, "space", within)
    packed = pack(pltpu.with_memory_space_constraint(held, pltpu.VMEM))
    far, near, packed = lax.optimization_barrier((far, near, packed))
    packed = patch(packed, far, near)
    packed, op_main, op_mass = lax.optimization_barrier((packed, op_main, op_mass))
    recv = lax.all_to_all(packed, "tm", 0, 0).reshape(LENGTH, BOX)
    ops = select_ops(jnp.transpose(op_main, (1, 2, 0)), jnp.transpose(op_mass, (1, 2, 0)))
    ops, jac = lax.optimization_barrier((ops, jac))
    box = select_jac(jac, far, near)
    sent = solve(recv, ops, box)
    back = lax.all_to_all(sent, "tm", 0, 0)
    return unpack(back)


def solution(mesh):
    in_specs = (
        P("tm", "space"),
        P("space", None, None),
        P("space", None, None),
        P("space", None, None),
    )
    out_specs = (P("tm", "space"), P("tm", "space"), P("tm", "space"))
    return jax.shard_map(
        per_device, mesh=mesh, in_specs=in_specs, out_specs=out_specs, check_vma=False
    )
```

```python
import functools
import math

import jax
import jax.numpy as jnp
import ml_dtypes
import numpy as np
from jax import lax
from jax.experimental import pallas as pl
from jax.experimental.pallas import tpu as pltpu
from jax.sharding import PartitionSpec as P

LENGTH = 256
PARTS = 16
STEPS = LENGTH // PARTS
BS = 64
LAYER = 1024
ROW = 256
LAYERS = 8
SLAB = LAYERS * LAYER
BLOCKS = SLAB // BS
SLOTS = 7
COL = 128
OWN = 4 * COL
BOX = 12 * COL
CHUNK = 16

ALPHA = 0.25
LOG_STEP = math.log(ALPHA) / LENGTH
MODULUS = ALPHA ** (1.0 / LENGTH)

f32 = jnp.float32
bf16 = jnp.bfloat16


def box_of(part):
    return part // 4, part // 2 % 2, part % 2


def dft_table():
    freq = np.arange(LENGTH)[:, None]
    step = np.arange(LENGTH)[None, :]
    angle = 2.0 * np.pi * (freq * step % LENGTH) / LENGTH
    table = np.stack([np.cos(angle), -np.sin(angle)], 1) / math.sqrt(LENGTH)
    table = table.reshape(PARTS, STEPS, 2, LENGTH).transpose(0, 2, 1, 3)
    table = table.reshape(2 * LENGTH, LENGTH)
    high = table.astype(ml_dtypes.bfloat16)
    low = (table - high.astype(np.float64)).astype(ml_dtypes.bfloat16)
    return np.concatenate([high, high, low], axis=1)


def step_ids(part, count, width):
    return part * STEPS + lax.broadcasted_iota(jnp.int32, (count, width), 0)


def cost(flops, nbytes):
    return pl.CostEstimate(flops=flops, bytes_accessed=nbytes, transcendentals=0)


def dot(a, b):
    return jnp.dot(a, b, preferred_element_type=f32)


def scales():
    ids = step_ids(lax.axis_index("tm"), STEPS, COL).astype(f32)
    return jnp.exp(ids * LOG_STEP)


def pack_kernel(forcing, out):
    scale = scales()
    half = lax.broadcasted_iota(jnp.int32, (STEPS, COL), 1) < BS

    def column(z, y, x):
        at = z * LAYER + y * ROW + x * COL
        return forcing[:, at : at + COL] * scale

    def put(dest, c, value):
        out[dest, :, c * COL : (c + 1) * COL] = value.astype(bf16)

    for dest in range(PARTS):
        zg, yg, xg = box_of(dest)
        for d in range(2):
            for e in range(2):
                put(dest, 2 * d + e, column(2 * zg + d, 2 * yg + e, xg))
            y = 2 * yg + d
            if zg > 0:
                put(dest, 4 + d, column(2 * zg - 1, y, xg))
            if zg < 3:
                put(dest, 6 + d, column(2 * zg + 2, y, xg))
            z = 2 * zg + d
            put(dest, 8 + d, column(z, 2 - yg, xg))
            first = column(z, 2 * yg, 1 - xg)
            second = column(z, 2 * yg + 1, 1 - xg)
            if xg == 0:
                pair = jnp.where(half, first, pltpu.roll(second, BS, 1))
            else:
                pair = jnp.where(half, pltpu.roll(first, BS, 1), second)
            put(dest, 10 + d, pair)


def pack(forcing):
    return pl.pallas_call(
        pack_kernel,
        in_specs=[pl.BlockSpec(memory_space=pltpu.VMEM)],
        out_shape=jax.ShapeDtypeStruct((PARTS, STEPS, BOX), bf16),
        name="pack",
        compiler_params=pltpu.CompilerParams(vmem_limit_bytes=6 * 2**20),
        cost_estimate=cost(10**6, 4 * 10**6),
    )(forcing)


def patch_kernel(packed, far, near, out, sems):
    def place(low_edge, high_edge):
        copies = [
            pltpu.make_async_copy(
                edge.at[pl.ds(0, 4)],
                out.at[pl.ds(first_dest, 4), :, pl.ds(first * COL, 2 * COL)],
                sems.at[which],
            )
            for which, (edge, first_dest, first) in enumerate(
                ((low_edge, 0, 4), (high_edge, PARTS - 4, 6))
            )
        ]
        for copy in copies:
            copy.start()
        for copy in copies:
            copy.wait()

    core = lax.axis_index("space") % 2

    @pl.when(core == 0)
    def _():
        place(far, near)

    @pl.when(core == 1)
    def _():
        place(near, far)


def patch(packed, far, near):
    anywhere = pl.BlockSpec(memory_space=pl.ANY)
    return pl.pallas_call(
        patch_kernel,
        in_specs=[anywhere] * 3,
        out_specs=anywhere,
        out_shape=jax.ShapeDtypeStruct((PARTS, STEPS, BOX), bf16),
        scratch_shapes=[pltpu.SemaphoreType.DMA((2,))],
        input_output_aliases={0: 0},
        name="patch",
        compiler_params=pltpu.CompilerParams(vmem_limit_bytes=2**20),
        cost_estimate=cost(10**3, 2 * 10**5),
    )(packed, far, near)


def selector(blocks, width):
    block = lax.broadcasted_iota(jnp.int32, (BLOCKS, width), 0)
    lane = lax.broadcasted_iota(jnp.int32, (BLOCKS, width), 1)
    hit = block == blocks
    pieces = [
        jnp.where(hit & (lane % CHUNK == o), 1.0, 0.0).astype(bf16) for o in range(CHUNK)
    ]
    return jnp.concatenate(pieces, axis=0)


def reorder(width):
    slots = width // BS
    source = lax.broadcasted_iota(jnp.int32, (width, width), 0)
    lane = lax.broadcasted_iota(jnp.int32, (width, width), 1)
    wanted = lane % BS // CHUNK * (slots * CHUNK) + lane // BS * CHUNK + lane % CHUNK
    return jnp.where(source == wanted, 1.0, 0.0).astype(bf16)


def select_chunk(read, chosen):
    rows = jnp.concatenate([read(o) for o in range(CHUNK)], axis=1)
    return dot(rows, chosen).astype(bf16)


def select_all(jac, chosen, perm):
    chunks = BS // CHUNK
    rows = jnp.concatenate(
        [
            jnp.concatenate([jac[c * CHUNK + o] for c in range(chunks)], axis=0)
            for o in range(CHUNK)
        ],
        axis=1,
    )
    picked = dot(rows, chosen).astype(bf16)
    side = jnp.concatenate([picked[c * BS : (c + 1) * BS] for c in range(chunks)], axis=1)
    return dot(side, perm).astype(bf16)


def slots_of():
    return lax.broadcasted_iota(jnp.int32, (1, COL), 1) // CHUNK


def block_at(z, y, x):
    return z * 16 + y * 4 + x


def edge_kernel(forcing, jac, far, near, held, local, sems):
    _, yg, xg = box_of(lax.axis_index("tm"))
    near_layer = jnp.where(lax.axis_index("space") % 2 == 0, LAYERS - 1, 0)
    first, middle, last = LAYER, SLAB - 2 * LAYER, LAYER
    cuts = [pl.ds(0, first), pl.ds(SLAB - last, last), pl.ds(first, middle)]
    copies = [
        pltpu.make_async_copy(forcing.at[:, cut], held.at[:, cut], sems.at[which])
        for which, cut in enumerate(cuts)
    ]
    for c in range(BS // CHUNK):
        cut = pl.ds(c * CHUNK, CHUNK)
        copies.append(pltpu.make_async_copy(jac.at[cut], local.at[cut], sems.at[3 + c]))
    for which in (3, 4, 5, 6, 0, 1, 2):
        copies[which].start()
    scale = scales()
    slot = slots_of()
    layer = jnp.where(slot < 4, near_layer, LAYERS - 1 - near_layer)
    chosen = selector(
        block_at(layer, 2 * yg + slot // 2 % 2, 2 * xg + slot % 2), COL
    )
    perm = reorder(4 * COL)
    copies[0].wait()
    copies[1].wait()
    even = near_layer > 0
    for target in range(4):
        for d in range(2):
            at = (2 * (target // 2) + d) * ROW + target % 2 * COL
            to = slice(d * COL, (d + 1) * COL)
            bottom = (held[:, at : at + COL] * scale).astype(bf16)
            at += SLAB - LAYER
            top = (held[:, at : at + COL] * scale).astype(bf16)
            near[target, :, to] = jnp.where(even, top, bottom)
            far[target, :, to] = jnp.where(even, bottom, top)
    for c in range(BS // CHUNK):
        copies[3 + c].wait()
    picked = select_all(local, chosen, perm)
    for a in range(BS // STEPS):
        rows = slice(a * STEPS, (a + 1) * STEPS)
        near[4 + a] = picked[rows, : 2 * COL]
        far[4 + a] = picked[rows, 2 * COL :]
    copies[2].wait()


def edges(forcing, jac):
    edge = jax.ShapeDtypeStruct((4 + BS // STEPS, STEPS, 2 * COL), bf16)
    hbm = pl.BlockSpec(memory_space=pltpu.HBM)
    return pl.pallas_call(
        edge_kernel,
        in_specs=[hbm, hbm],
        out_shape=(edge, edge, jax.ShapeDtypeStruct((STEPS, SLAB), f32)),
        scratch_shapes=[
            pltpu.VMEM((BS, BS, BLOCKS), bf16),
            pltpu.SemaphoreType.DMA((7,)),
        ],
        name="edges",
        compiler_params=pltpu.CompilerParams(vmem_limit_bytes=6 * 2**20),
        cost_estimate=cost(10**8, 2 * 10**6),
    )(forcing, jac)


def jac_kernel(jac, far, near, box, local, sem):
    copy = pltpu.make_async_copy(jac, local, sem)
    copy.start()
    zg, yg, xg = box_of(lax.axis_index("tm"))
    slot = slots_of()
    d = slot // 2 % 2
    e = slot % 2
    first = slot < 4
    own = block_at(2 * zg + slot // 4, 2 * yg + d, 2 * xg + e)
    layer = jnp.where(
        first, jnp.maximum(2 * zg - 1, 0), jnp.minimum(2 * zg + 2, LAYERS - 1)
    )
    faces = block_at(layer, 2 * yg + d, 2 * xg + e)
    beside = block_at(2 * zg + d, 2 - yg, 2 * xg + e)
    ahead = block_at(2 * zg + d, 2 * yg + e, 2 - xg)
    perm = reorder(4 * COL)
    copy.wait()
    even = lax.axis_index("space") % 2 == 0

    def other(edge):
        return jnp.concatenate([edge[4 + a] for a in range(BS // STEPS)], axis=0)

    near, far = other(near), other(far)
    for at, blocks in enumerate((own, faces, jnp.where(first, beside, ahead))):
        both = select_all(local, selector(blocks, COL), perm)
        for which in range(2):
            value = both[:, which * 2 * COL : (which + 1) * 2 * COL]
            if at == 1 and which == 0:
                value = jnp.where(zg == 0, jnp.where(even, far, near), value)
            if at == 1 and which == 1:
                value = jnp.where(zg == 3, jnp.where(even, near, far), value)
            p = 2 * at + which
            box[:, 2 * p * COL : 2 * (p + 1) * COL] = value


def select_jac(jac, far, near):
    vmem = pl.BlockSpec(memory_space=pltpu.VMEM)
    return pl.pallas_call(
        jac_kernel,
        in_specs=[pl.BlockSpec(memory_space=pltpu.HBM), vmem, vmem],
        out_shape=jax.ShapeDtypeStruct((BS, BOX), bf16),
        scratch_shapes=[pltpu.VMEM((BS, BS, BLOCKS), bf16), pltpu.SemaphoreType.DMA],
        name="select_jac",
        compiler_params=pltpu.CompilerParams(vmem_limit_bytes=8 * 2**20),
        cost_estimate=cost(10**9, 2 * 10**6),
    )(jac, far, near)


def ops_kernel(main, mass, out, chosen, picked):
    step = pl.program_id(0)
    zg, yg, xg = box_of(lax.axis_index("tm"))

    @pl.when(step == 0)
    def _():
        slot = slots_of()
        blocks = block_at(2 * zg + slot // 4, 2 * yg + slot // 2 % 2, 2 * xg + slot % 2)
        chosen[...] = selector(blocks, COL)

    for which, source in enumerate((main, mass)):
        picked[which, step] = select_chunk(lambda o: source[o], chosen[...])

    @pl.when(step == BS // CHUNK - 1)
    def _():
        perm = reorder(4 * COL)
        both = [
            dot(
                jnp.concatenate([picked[which, c] for c in range(BS // CHUNK)], axis=1), perm
            )
            for which in range(2)
        ]
        lane = lax.broadcasted_iota(jnp.int32, (BS, 2 * COL), 1)
        low = lane % COL < BS
        zero = jnp.zeros((BS, 2 * COL), f32)
        for dz in range(2):
            for dy in range(2):
                pair = 2 * dz + dy
                cut = slice(pair * COL, (pair + 1) * COL)
                slots = [
                    jnp.concatenate([b[s * BS : (s + 1) * BS, cut] for b in both], axis=1)
                    for s in range(SLOTS)
                ]

                def put(at, value):
                    out[pair, at * BS : (at + 1) * BS] = value.astype(bf16)

                def diagonal(at, value):
                    put(at, jnp.where(low, value, zero))
                    put(at + 1, jnp.where(low, zero, value))

                put(0, jnp.where(low, slots[0], slots[1]))
                put(1, jnp.where(low, slots[2], slots[0]))
                diagonal(2, slots[6 - dz])
                diagonal(4, slots[4 - dy])
                diagonal(6, slots[5 + dz])
                faces = (yg == 1) if dy == 0 else (yg == 0)
                diagonal(8, slots[3 + dy] * jnp.where(faces, 1.0, 0.0))
                after = jnp.where(xg == 0, 1.0, 0.0)
                put(
                    10 + dy,
                    jnp.where(low, slots[1] * (1.0 - after), slots[2] * after),
                )
                put(11 - dy, zero)


def select_ops(main, mass):
    spec = pl.BlockSpec((CHUNK, SLOTS * BS, BLOCKS), lambda c: (c, 0, 0))
    return pl.pallas_call(
        ops_kernel,
        grid=(BS // CHUNK,),
        in_specs=[spec, spec],
        out_specs=pl.BlockSpec((4, 6 * COL, 2 * COL), lambda c: (0, 0, 0)),
        out_shape=jax.ShapeDtypeStruct((4, 6 * COL, 2 * COL), bf16),
        scratch_shapes=[
            pltpu.VMEM((CHUNK * BLOCKS, COL), bf16),
            pltpu.VMEM((2, BS // CHUNK, SLOTS * BS, COL), bf16),
        ],
        name="select_ops",
        compiler_params=pltpu.CompilerParams(vmem_limit_bytes=52 * 2**20),
        cost_estimate=cost(4 * 10**9, 16 * 10**6),
    )(main, mass)


def solve_kernel(recv, ops, box, table, out):
    lane = lax.broadcasted_iota(jnp.int32, (BS, 2 * COL), 1) // BS

    def diagonal(p):
        value = box[:, 2 * p * COL : 2 * (p + 1) * COL]
        rows = [jnp.where(lane == q, value, jnp.zeros_like(value)) for q in range(4)]
        return jnp.concatenate(rows, axis=0)

    diagonals = [diagonal(p) for p in range(6)]

    def fields(c, count):
        return recv[:, c * COL : (c + count) * COL]

    firsts = [dot(fields(2 * p, 2), diagonals[p]) for p in range(2)]
    halves = [value.astype(bf16) for value in firsts]
    halves += [dot(fields(2 * p, 2), diagonals[p]).astype(bf16) for p in range(2, 6)]
    lows = [half[:, e * COL : (e + 1) * COL] for half in halves for e in range(2)]

    seconds = []
    for dz in range(2):
        residues = []
        for dy in range(2):
            pair = 2 * dz + dy
            around = jnp.concatenate(
                [
                    lows[pair],
                    lows[2 - 2 * dz + dy],
                    lows[2 * dz + 1 - dy],
                    lows[4 + 2 * dz + dy],
                    lows[8 + dz],
                    lows[10 + dz],
                ],
                axis=1,
            )
            image = dot(around, ops[pair])
            earlier = pltpu.roll(image[:, COL:], 1, 0)
            residue = fields(pair, 1).astype(f32) - image[:, :COL] + MODULUS * earlier
            residues.append(residue.astype(bf16))
        second = firsts[dz] + dot(jnp.concatenate(residues, axis=1), diagonals[dz])
        in_time = second.astype(bf16)
        for dest in range(PARTS):
            out[dest, 2 * STEPS :, 2 * dz * COL : 2 * (dz + 1) * COL] = in_time[
                dest * STEPS : (dest + 1) * STEPS
            ]
        seconds.append(second)
    second = jnp.concatenate(seconds, axis=1)
    high = second.astype(bf16)
    rest = (second - high.astype(f32)).astype(bf16)
    spectrum = dot(table[...], jnp.concatenate([high, rest, high], axis=0)).astype(bf16)
    for dest in range(PARTS):
        out[dest, : 2 * STEPS] = spectrum[dest * 2 * STEPS : (dest + 1) * 2 * STEPS]


def solve(recv, ops, box):
    return pl.pallas_call(
        solve_kernel,
        out_shape=jax.ShapeDtypeStruct((PARTS, 3 * STEPS, OWN), bf16),
        name="solve",
        compiler_params=pltpu.CompilerParams(vmem_limit_bytes=16 * 2**20),
        cost_estimate=cost(3 * 10**9, 5 * 10**6),
    )(recv, ops, box, jnp.asarray(dft_table()))


def unpack_kernel(recv, real, imag, in_time, ready, sems):
    ids = step_ids(lax.axis_index("tm"), STEPS, COL).astype(f32)
    growth = jnp.exp(ids * -LOG_STEP)
    copies = []
    for z in range(LAYERS):
        zg, d = z // 2, z % 2
        for which, out in enumerate((real, imag, in_time)):
            for rest in range(4):
                source = 4 * zg + rest
                _, yg, xg = box_of(source)
                for e in range(2):
                    at = z * LAYER + (2 * yg + e) * ROW + xg * COL
                    c = 2 * d + e
                    value = recv[
                        source,
                        which * STEPS : (which + 1) * STEPS,
                        c * COL : (c + 1) * COL,
                    ].astype(f32)
                    ready[which, :, at : at + COL] = (
                        value * growth if which == 2 else value
                    )
            cut = pl.ds(z * LAYER, LAYER)
            copy = pltpu.make_async_copy(
                ready.at[which, :, cut], out.at[:, cut], sems.at[len(copies)]
            )
            copy.start()
            copies.append(copy)
    for copy in copies:
        copy.wait()


def unpack(recv):
    out = jax.ShapeDtypeStruct((STEPS, SLAB), f32)
    return pl.pallas_call(
        unpack_kernel,
        out_shape=(out, out, out),
        out_specs=(pl.BlockSpec(memory_space=pltpu.HBM),) * 3,
        scratch_shapes=[pltpu.VMEM((3, STEPS, SLAB), f32), pltpu.SemaphoreType.DMA((24,))],
        name="unpack",
        compiler_params=pltpu.CompilerParams(vmem_limit_bytes=6 * 2**20),
        cost_estimate=cost(10**6, 3 * 10**6),
    )(recv)


def per_device(forcing, op_main, op_mass, jacobi_inv):
    count = lax.axis_size("space")
    across = [(i, i + 1) for i in range(1, count - 1, 2)]
    within = [(i, i + 1) for i in range(0, count, 2)]
    across += [(j, i) for i, j in across]
    within += [(j, i) for i, j in within]
    jac = jnp.transpose(jacobi_inv, (1, 2, 0))
    forcing = pltpu.with_memory_space_constraint(forcing, pltpu.HBM)
    far, near, held = edges(forcing, pltpu.with_memory_space_constraint(jac, pltpu.HBM))
    far = lax.ppermute(far, "space", across)
    near = lax.ppermute(near, "space", within)
    packed = pack(pltpu.with_memory_space_constraint(held, pltpu.VMEM))
    far, near, packed = lax.optimization_barrier((far, near, packed))
    packed = patch(packed, far, near)
    packed, op_main, op_mass = lax.optimization_barrier((packed, op_main, op_mass))
    recv = lax.all_to_all(packed, "tm", 0, 0).reshape(LENGTH, BOX)
    ops = select_ops(jnp.transpose(op_main, (1, 2, 0)), jnp.transpose(op_mass, (1, 2, 0)))
    ops, jac = lax.optimization_barrier((ops, jac))
    box = select_jac(jac, far, near)
    sent = solve(recv, ops, box)
    back = lax.all_to_all(sent, "tm", 0, 0)
    return unpack(back)


def solution(mesh):
    in_specs = (
        P("tm", "space"),
        P("space", None, None),
        P("space", None, None),
        P("space", None, None),
    )
    out_specs = (P("tm", "space"), P("tm", "space"), P("tm", "space"))
    return jax.shard_map(
        per_device, mesh=mesh, in_specs=in_specs, out_specs=out_specs, check_vma=False
    )
```
